256 devices in a mesh: mem: 16 (over z, core), tile: 16 (over x, y).
Axes of the slice: x: 4, y: 4, z: 8, core: 2. Of those that a mesh axis runs over, the one named last changes fastest.
Arguments:
- members: float32 [512, 2, 512, 128], P('mem', None, 'tile'), may hold values from -6 to 6
- courant: float32 [2, 128], replicated, may hold values from 0.2 to 0.9
- obs_cell: int32 [4096], P('tile'), may hold values from 0 to 8191
- obs_value: float32 [4096], P('tile'), may hold values from -6 to 6
- obs_rinv: float32 [4096], P('tile'), may hold values from 0.3 to 3
- nbr_obs: int32 [512, 512], P(('tile', 'mem')), may hold values from 0 to 4095, as said below
- nbr_class: int32 [512, 512], P(('tile', 'mem')), may hold values from 0 to 15
- nbr_count: int32 [512], P(('tile', 'mem')), may hold values from 128 to 512, as said below
- loc_table: float32 [16], replicated, may hold values from 0.2 to 1
Outputs:
- analysis: float32 [512, 2, 512, 128], P('mem', None, 'tile')
The draws below stay inside these ranges and needn't reach their ends.
Inputs may be any that keep to these rules, and one draw needn't show every extreme that they name: nbr_obs[g] names observations of the tile of longitude line g or of the tiles just west and east of it (periodic); an observation may be named more than once. Only the first nbr_count[g] slots of patch g are used.
All inputs are finite; a program needn't handle non-finite values. Where the reference program divides by a largest or mean magnitude, that divisor is 1e-20 or more.
Results may differ from the reference program's by a relative error of at most 0.0003.
Values sent between devices are 32-bit elements; how exact they have to be, the bound alone decides.
No kernel may reach another device: no remote copies, remote signals or barrier semaphores. Data moves between devices by JAX's collectives and lax.ppermute only.
A program may use at most 64 MiB of HBM per device.

```python
import math
import jax
import jax.numpy as jnp
from jax import lax

K = 512
LEV = 2
NLAT = 128
OBS_T = 256
NNB = 512
NCLASS = 16
NSTEP = 2
NS_ITERS = 8
LON_T = 32
NLON = 512
NOBS = 4096


def neighbour_slots(key):
    return jax.random.randint(key, (NLON, NNB), 0, 3 * OBS_T)


def draw_nbr_obs(key, part):
    local = neighbour_slots(key)
    tiles = NOBS // OBS_T
    row_tile = (jnp.arange(NLON) // LON_T)[:, None]
    return ((row_tile - 1 + local // OBS_T) % tiles * OBS_T + local % OBS_T).astype(jnp.int32)


def draw_nbr_class(key, part):
    local = neighbour_slots(key)
    key = jax.random.fold_in(key, 12)
    base = jnp.where(local // OBS_T == 1, 0, NCLASS // 2)
    return (base + jax.random.randint(key, (NLON, NNB), 0, NCLASS // 2)).astype(jnp.int32)


def draw_nbr_count(key, part):
    key = jax.random.fold_in(key, 13)
    first, second = jax.random.split(key)
    counts = jax.random.randint(first, (NLON,), NNB // 4, NNB + 1)
    chosen = jax.random.randint(second, (), 0, NLON)
    return jnp.where(jnp.arange(NLON) == chosen, NNB, counts).astype(jnp.int32)


def plant(array, own_key, low, top_value):
    longest = array.shape.index(max(array.shape))
    spots = []
    for shift in (0, 1):
        where = [jax.random.randint(jax.random.fold_in(own_key, axis), (), 0, length) for axis, length in enumerate(array.shape)]
        where[longest] = (where[longest] + shift) % array.shape[longest]
        spots.append(tuple(where))
    return array.at[spots[0]].set(low).at[spots[1]].set(top_value)


def block_scale(own_key, extent, pieces, smallest, high):
    level, own = 1.0, jax.random.fold_in(own_key, 6)
    for dim, parts in pieces:
        steps = jnp.exp(jax.random.uniform(jax.random.fold_in(own, dim), (parts,), jnp.float32, smallest / len(pieces), high / len(pieces)))
        level = level * jnp.repeat(steps, extent[dim] // parts).reshape([-1 if axis == dim else 1 for axis in range(len(extent))])
    return level


def gaussian(key, extent, deviation, reach, cuts=(), held_as=jnp.bfloat16):
    loudness = block_scale(key, extent, cuts, -0.22, 0.18) if cuts else 1.0
    values = jax.random.normal(key, extent, jnp.float32) * deviation * loudness
    return jnp.minimum(jnp.maximum(values, -reach), reach).astype(held_as)


def setup_inputs(seed: int = 0) -> dict:
    seeds = jax.random.split(jax.random.key(seed), 10)
    members = gaussian(seeds[0], (K, LEV, NLON, NLAT), 1.0, 6.0, ((0, 16), (2, 16)), jnp.float32)
    courant = jnp.clip(jax.random.uniform(seeds[1], (LEV, NLAT), jnp.float32, 0.2, 0.9), 0.2, 0.9)
    obs_cell = plant(jax.random.randint(seeds[2], (NOBS,), 0, LEV * LON_T * NLAT), jax.random.fold_in(seeds[2], 1), 0, (LEV * LON_T * NLAT) - 1).astype(jnp.int32)
    obs_value = gaussian(seeds[3], (NOBS,), 1.0, 6.0, ((0, 16),), jnp.float32)
    obs_rinv = jnp.clip(jnp.exp(math.log(3.0) - 2.3025851 * jax.random.uniform(seeds[4], (NOBS,), jnp.float32) ** block_scale(seeds[4], (NOBS,), ((0, 16),), -0.2, 0.2)), 0.3, 3.0)
    nbr_obs = draw_nbr_obs(jax.random.fold_in(seeds[9], 71), 0)
    nbr_class = draw_nbr_class(jax.random.fold_in(seeds[9], 71), 0)
    nbr_count = draw_nbr_count(jax.random.fold_in(seeds[9], 71), 0)
    loc_table = jnp.clip(jax.random.uniform(seeds[8], (NCLASS,), jnp.float32, 0.2, 1.0), 0.2, 1.0)
    return {"members": members, "courant": courant, "obs_cell": obs_cell, "obs_value": obs_value, "obs_rinv": obs_rinv, "nbr_obs": nbr_obs, "nbr_class": nbr_class, "nbr_count": nbr_count, "loc_table": loc_table}


DIFFUSE = 0.1
HIGH = lax.Precision.HIGHEST

def advance(field, west, courant):
    upper = jnp.concatenate([field[..., 1:], field[..., -1:]], -1)
    lower = jnp.concatenate([field[..., :1], field[..., :-1]], -1)
    return field - courant[None, :, None, :] * (field - west) + DIFFUSE * (upper + lower - 2.0 * field)

def inverse_root(matrix):
    eye = jnp.eye(matrix.shape[0], dtype=jnp.float32)
    scale = jnp.max(lax.optimization_barrier(jnp.sum(jnp.abs(matrix), 1)))
    current = matrix / scale
    inverse = eye
    for sweep in range(NS_ITERS):
        factor = 0.5 * (3.0 * eye - jnp.dot(inverse, current, precision=HIGH))
        if sweep + 1 < NS_ITERS:
            current = jnp.dot(current, factor, precision=HIGH)
        inverse = jnp.dot(factor, inverse, precision=HIGH)
    return (inverse, scale)

def finish(gram, rhs):
    eye = jnp.eye(gram.shape[0], dtype=jnp.float32)
    inverse, scale = inverse_root(eye + gram)
    mean_w = jnp.dot(inverse, jnp.dot(inverse, rhs, precision=HIGH), precision=HIGH) / scale
    return mean_w[:, None] + inverse / jnp.sqrt(scale)

def reference(members, courant, obs_cell, obs_value, obs_rinv, nbr_obs, nbr_class, nbr_count, loc_table):
    field = members
    for section in range(NSTEP):
        field = advance(field, jnp.roll(field, 1, axis=2), courant)
    obs_tile = (jnp.arange(NOBS) // OBS_T).astype(jnp.int32)
    level = obs_cell // (LON_T * NLAT)
    rest = obs_cell % (LON_T * NLAT)
    line = obs_tile * LON_T + rest // NLAT
    flat = ((level * NLON + line) * NLAT + rest % NLAT).astype(jnp.int32)
    ens_obs = field.reshape(K, -1)[:, flat]
    obs_mean = lax.optimization_barrier(jnp.mean(ens_obs, axis=0))
    obs_pert = ens_obs - obs_mean[None, :]
    innov = obs_value - obs_mean
    classes = jnp.arange(NCLASS).astype(jnp.int32)

    def patch(index):
        ids = nbr_obs[index]
        local_w = lax.optimization_barrier(jnp.sum(jnp.where(nbr_class[index][:, None] == classes[None, :], loc_table[None, :], 0.0), 1))
        weight = jnp.where(jnp.arange(NNB) < nbr_count[index], obs_rinv[ids] * local_w, 0.0)
        listed = obs_pert[:, ids]
        gram = jnp.dot(listed * weight[None, :], listed.T, precision=HIGH) / (K - 1)
        rhs = jnp.dot(listed, weight * innov[ids], precision=HIGH) / (K - 1)
        transform = finish(gram, rhs)
        column = jnp.take(field, index, axis=2).reshape(K, LEV * NLAT)
        center = lax.optimization_barrier(jnp.mean(column, axis=0))
        result = center[None, :] + jnp.dot(transform.T, column - center[None, :], precision=HIGH)
        return result.reshape(K, LEV, NLAT)
    stacked = lax.map(patch, jnp.arange(NLON).astype(jnp.int32))
    return jnp.transpose(stacked, (1, 2, 0, 3))
```

```python
import jax
import jax.numpy as jnp
from jax import lax
from jax.experimental import pallas as pl
from jax.experimental.pallas import tpu as pltpu
from jax.sharding import PartitionSpec as P

NSTEP = 2
NS_ITERS = 8
DIFFUSE = 0.1
HALF = 256
PAD = 16
BF = jnp.bfloat16
F32 = jnp.float32


def split(value):
    high = value.astype(BF)
    return high, (value - high.astype(F32)).astype(BF)


def mm(left, right):
    return jnp.dot(left, right, preferred_element_type=F32)


def mm_t(left, right):
    return lax.dot_general(left, right, (((1,), (1,)), ((), ())), preferred_element_type=F32)


def analyse_kernel(pool_ref, side_ref, wsum_ref, cols_ref, out_ref, bh, bl, t, p, ph, pl_, gh, gl, v, vh, vl):
    members, nobs = pool_ref.shape
    levels, nlat = cols_ref.shape[1], cols_ref.shape[3]
    states = levels * nlat
    lo, hi = slice(0, HALF), slice(HALF, 2 * HALF)
    mean = jnp.sum(pool_ref[...], axis=0, keepdims=True) * (1.0 / members)
    total = side_ref[1:2, :] * wsum_ref[...]
    root = jnp.where(total > 0.0, jnp.sqrt(jnp.maximum(total, 1e-30)), 0.0)
    row = jnp.broadcast_to(root * (side_ref[0:1, :] - mean), (PAD, nobs))
    bh[0:PAD, :], bh[PAD : 2 * PAD, :] = split(row)
    high, low = split((pool_ref[...] - mean) * root)
    bh[2 * PAD :, :] = high
    bl[...] = low
    first = bh[0 : 2 * PAD + HALF, :]
    second = bh[2 * PAD + HALF :, :]
    top = 2 * PAD
    inv = 1.0 / (members - 1)
    left = mm_t(first, first[top:, :])
    right = mm_t(first, second)
    left_low = mm_t(first, bl[lo, :])
    right_low = mm_t(first, bl[hi, :])
    t[lo, lo] = 0.5 * left[top:] + left_low[top:]
    t[lo, hi] = right[top:] + right_low[top:]
    rhs0 = (left[0:1] + left[PAD : PAD + 1] + left_low[0:1]) * inv
    rhs1 = (right[0:1] + right[PAD : PAD + 1] + right_low[0:1]) * inv
    t[hi, lo] = mm_t(second, bl[lo, :])
    t[hi, hi] = 0.5 * mm_t(second, second) + mm_t(second, bl[hi, :])
    g00 = (t[lo, lo] + t[lo, lo].T) * inv
    g01 = (t[lo, hi] + t[hi, lo].T) * inv
    g11 = (t[hi, hi] + t[hi, hi].T) * inv
    eye = (
        lax.broadcasted_iota(jnp.int32, (HALF, HALF), 0)
        == lax.broadcasted_iota(jnp.int32, (HALF, HALF), 1)
    ).astype(F32)
    g00 = g00 + eye
    g11 = g11 + eye
    g10 = g01.T
    rows0 = jnp.sum(jnp.abs(g00), 0, keepdims=True) + jnp.sum(jnp.abs(g10), 0, keepdims=True)
    rows1 = jnp.sum(jnp.abs(g01), 0, keepdims=True) + jnp.sum(jnp.abs(g11), 0, keepdims=True)
    scale = jnp.max(jnp.maximum(rows0, rows1), axis=1, keepdims=True)
    shrink = 1.0 / scale
    v[states:, lo] = jnp.broadcast_to(rhs0, (PAD, HALF))
    v[states:, hi] = jnp.broadcast_to(rhs1, (PAD, HALF))

    def put(rows, cols, value):
        p[rows, cols] = value
        ph[rows, cols], pl_[rows, cols] = split(value)

    put(lo, lo, g00 * shrink)
    put(lo, hi, g01 * shrink)
    put(hi, lo, g10 * shrink)
    put(hi, hi, g11 * shrink)
    for lev in range(levels):
        block = cols_ref[:, lev, :, :].reshape(members, nlat).T
        v[lev * nlat : (lev + 1) * nlat, :] = block
    center = jnp.sum(v[0:states, :], axis=1, keepdims=True) * (1.0 / members)
    v[0:states, :] = v[0:states, :] - center

    def factor():
        vh[...], vl[...] = split(v[...])
        for cols in (lo, hi):
            part = mm(vh[...], ph[:, cols]) + mm(vl[...], ph[:, cols]) + mm(vh[...], pl_[:, cols])
            v[:, cols] = 1.5 * v[:, cols] - 0.5 * part

    def step(_, carry):
        t[lo, lo] = 0.5 * mm(ph[lo, :], ph[:, lo]) + mm(ph[lo, :], pl_[:, lo])
        t[lo, hi] = mm(ph[lo, :], ph[:, hi]) + mm(ph[lo, :], pl_[:, hi])
        t[hi, lo] = mm(ph[hi, :], pl_[:, lo])
        t[hi, hi] = 0.5 * mm(ph[hi, :], ph[:, hi]) + mm(ph[hi, :], pl_[:, hi])
        g00 = t[lo, lo] + t[lo, lo].T
        g01 = t[lo, hi] + t[hi, lo].T
        g11 = t[hi, hi] + t[hi, hi].T
        g10 = g01.T
        gh[lo, lo], gl[lo, lo] = split(g00)
        gh[hi, lo], gl[hi, lo] = split(g10)
        gh[lo, hi], gl[lo, hi] = split(g01)
        gh[hi, hi], gl[hi, hi] = split(g11)
        factor()

        def cube(rows, cols):
            return (
                mm(ph[rows, :], gh[:, cols]) + mm(ph[rows, :], gl[:, cols]) + mm(pl_[rows, :], gh[:, cols])
            )

        n00 = 2.25 * p[lo, lo] - 1.5 * g00 + 0.25 * cube(lo, lo)
        n01 = 2.25 * p[lo, hi] - 1.5 * g01 + 0.25 * cube(lo, hi)
        n11 = 2.25 * p[hi, hi] - 1.5 * g11 + 0.25 * cube(hi, hi)
        put(lo, lo, n00)
        put(lo, hi, n01)
        put(hi, lo, n01.T)
        put(hi, hi, n11)
        return carry

    lax.fori_loop(0, NS_ITERS - 1, step, 0)
    factor()
    shift = jnp.sum(v[0:states, :] * v[states : states + 1, :], axis=1, keepdims=True) * shrink
    result = center + shift + v[0:states, :] * lax.rsqrt(scale)
    for lev in range(levels):
        block = result[lev * nlat : (lev + 1) * nlat, :].T
        out_ref[:, lev, :, :] = block.reshape(out_ref.shape[0], out_ref.shape[2], nlat)


def analyse(pool, side, wsum, cols, which):
    members, nobs = pool.shape
    devices, _, levels, mem_dev, nlat = cols.shape
    states = levels * nlat
    return pl.pallas_call(
        analyse_kernel,
        grid=(1,),
        out_shape=jax.ShapeDtypeStruct((devices, levels, mem_dev, nlat), F32),
        in_specs=[
            pl.BlockSpec((members, nobs), lambda i: (0, 0)),
            pl.BlockSpec(side.shape, lambda i: (0, 0)),
            pl.BlockSpec((None, 1, nobs), lambda i: (which, 0, 0)),
            pl.BlockSpec((devices, None, levels, mem_dev, nlat), lambda i: (0, which, 0, 0, 0)),
        ],
        out_specs=pl.BlockSpec((devices, levels, mem_dev, nlat), lambda i: (0, 0, 0, 0)),
        scratch_shapes=[
            pltpu.VMEM((2 * PAD + members, nobs), BF),
            pltpu.VMEM((members, nobs), BF),
            pltpu.VMEM((members, members), F32),
            pltpu.VMEM((members, members), F32),
            pltpu.VMEM((members, members), BF),
            pltpu.VMEM((members, members), BF),
            pltpu.VMEM((members, members), BF),
            pltpu.VMEM((members, members), BF),
            pltpu.VMEM((states + PAD, members), F32),
            pltpu.VMEM((states + PAD, members), BF),
            pltpu.VMEM((states + PAD, members), BF),
        ],
        compiler_params=pltpu.CompilerParams(vmem_limit_bytes=48 * 1024 * 1024),
        cost_estimate=pl.CostEstimate(flops=12 * 10**9, bytes_accessed=4 * 10**6, transcendentals=0),
    )(pool, side, wsum, cols)


def forecast_kernel(field_ref, halo_ref, courant_ref, cell_ref, out_ref, obs_ref):
    members, levels, lines, nlat = out_ref.shape[2], out_ref.shape[1], out_ref.shape[0], out_ref.shape[3]
    nobs = cell_ref.shape[1]
    lat = lax.broadcasted_iota(jnp.int32, (members, nlat), 1)
    cells = cell_ref[...]
    spot = (lax.broadcasted_iota(jnp.int32, (nlat, nobs), 0) == cells % nlat).astype(BF)
    spot2 = jnp.concatenate([spot, spot], 0)
    source_row = cells // nlat
    obs = jnp.zeros((members, nobs), F32)

    def advance(field, west, courant):
        upper = jnp.where(lat == nlat - 1, field, pltpu.roll(field, nlat - 1, 1))
        lower = jnp.where(lat == 0, field, pltpu.roll(field, 1, 1))
        return field - courant * (field - west) + DIFFUSE * (upper + lower - 2.0 * field)

    for lev in range(levels):
        courant = courant_ref[lev : lev + 1, :]
        before = halo_ref[0, lev]
        old = halo_ref[1, lev]
        old_next = advance(old, before, courant)
        for line in range(lines):
            now = field_ref[pl.ds(lev * lines + line, members, stride=levels * lines), :]
            now_next = advance(now, old, courant)
            done = advance(now_next, old_next, courant)
            out_ref[line, lev] = done
            picked = mm(jnp.concatenate(split(done), 1), spot2)
            obs = jnp.where(source_row == lev * lines + line, picked, obs)
            old, old_next = now, now_next
    obs_ref[...] = obs


def forecast(members, halo, courant, obs_cell):
    mem_dev, levels, lines, nlat = members.shape
    rows = mem_dev * levels * lines
    return pl.pallas_call(
        forecast_kernel,
        out_shape=(
            jax.ShapeDtypeStruct((lines, levels, mem_dev, nlat), F32),
            jax.ShapeDtypeStruct((mem_dev, obs_cell.shape[0]), F32),
        ),
        compiler_params=pltpu.CompilerParams(vmem_limit_bytes=24 * 1024 * 1024),
    )(members.reshape(rows, nlat), halo, courant, obs_cell.reshape(1, -1))


def restore_kernel(first_ref, second_ref, out_ref):
    devices, levels, mem_dev, nlat = first_ref.shape
    lines = 2 * devices
    for device in range(devices):
        for lev in range(levels):
            for part, ref in ((0, first_ref), (1, second_ref)):
                rows = pl.ds(lev * lines + 2 * device + part, mem_dev, stride=levels * lines)
                out_ref[rows, :] = ref[device, lev]


def restore(first, second):
    devices, levels, mem_dev, nlat = first.shape
    rows = mem_dev * levels * 2 * devices
    out = pl.pallas_call(
        restore_kernel,
        out_shape=jax.ShapeDtypeStruct((rows, nlat), F32),
        compiler_params=pltpu.CompilerParams(vmem_limit_bytes=24 * 1024 * 1024),
    )(first, second)
    return out.reshape(mem_dev, levels, 2 * devices, nlat)


def shifted(value, axis, steps):
    count = lax.axis_size(axis)
    pairs = [(source, (source + steps) % count) for source in range(count)]
    return lax.ppermute(value, axis, pairs)


def on_device(
    members, courant, obs_cell, obs_value, obs_rinv, nbr_obs, nbr_class, nbr_count, loc_table
):
    mem_dev, levels, lines, nlat = members.shape
    devices = lax.axis_size("mem")
    obs_tile = obs_cell.shape[0]
    slots = nbr_obs.shape[1]
    edge = jnp.transpose(members[:, :, lines - NSTEP :, :], (2, 1, 0, 3))
    halo = shifted(edge, "tile", 1)
    tile_index = lax.axis_index("tile")
    tile_count = lax.axis_size("tile")
    local_ids = (nbr_obs // obs_tile - tile_index + 1) % tile_count * obs_tile + nbr_obs % obs_tile
    classes = jnp.arange(loc_table.shape[0])
    local_w = jnp.sum(
        jnp.where(nbr_class[..., None] == classes, loc_table, 0.0), -1
    )
    local_w = jnp.where(jnp.arange(slots) < nbr_count[:, None], local_w, 0.0)
    places = jnp.arange(3 * obs_tile)
    wsum = jnp.sum(jnp.where(local_ids[:, :, None] == places, local_w[:, :, None], 0.0), 1)

    field, local_obs = forecast(members, halo, courant, obs_cell)
    side = jnp.concatenate([obs_value[None], obs_rinv[None], jnp.zeros((6, obs_tile), F32)], 0)
    message = jnp.concatenate([local_obs, side], 0)
    west = shifted(message, "tile", 1)
    east = shifted(message, "tile", -1)
    three = jnp.concatenate([west, message, east], 1)
    columns = lax.all_to_all(
        field.reshape(devices, lines // devices, levels, mem_dev, nlat), "mem", 0, 0, tiled=True
    )
    pool = lax.all_gather(three[:mem_dev], "mem", axis=0, tiled=True)
    side3 = three[mem_dev:]
    parts = []
    for which in range(lines // devices):
        part = analyse(pool, side3, wsum[:, None, :], columns, which)
        parts.append(lax.all_to_all(part, "mem", 0, 0, tiled=True))
    return restore(*parts)


def solution(mesh):
    return jax.shard_map(
        on_device,
        mesh=mesh,
        in_specs=(
            P("mem", None, "tile", None),
            P(),
            P("tile"),
            P("tile"),
            P("tile"),
            P(("tile", "mem"), None),
            P(("tile", "mem"), None),
            P(("tile", "mem")),
            P(),
        ),
        out_specs=P("mem", None, "tile", None),
        check_vma=False,
    )
```

```python
import functools
import jax
import jax.numpy as jnp
from jax import lax
from jax.experimental import pallas as pl
from jax.experimental.pallas import tpu as pltpu
from jax.sharding import PartitionSpec as P

NSTEP = 2
NS_ITERS = 8
DIFFUSE = 0.1
HALF = 256
PAD = 16
NARROW = 32.0
SMALL, MID, LOW = 1.0 / 5, 1.0 / 32, 1.0 / 1024
BF = jnp.bfloat16
F32 = jnp.float32
LO, HI = slice(0, HALF), slice(HALF, 2 * HALF)


def split(value):
    high = value.astype(BF)
    return high, (value - high.astype(F32)).astype(BF)


def mm(left, right):
    return jnp.dot(left, right, preferred_element_type=F32)


def mm_t(left, right):
    return lax.dot_general(left, right, (((1,), (1,)), ((), ())), preferred_element_type=F32)


def root_kernel(near_ref, own_ref, far_ref, wsum_ref, out_ref, rhs_ref, bh, bl, t, p, ph, pl_, gh, gl, z, zh, zl):
    devices, _, obs_tile = own_ref.shape
    patches, members = out_ref.shape[:2]
    mem_dev = members // devices
    inv = 1.0 / (members - 1)
    top = 2 * PAD
    eye = (
        lax.broadcasted_iota(jnp.int32, (HALF, HALF), 0)
        == lax.broadcasted_iota(jnp.int32, (HALF, HALF), 1)
    ).astype(F32)

    def put(value, full, high, low, n, rows, cols):
        if full is not None:
            full[n, rows, cols] = value
        high[n, rows, cols], low[n, rows, cols] = split(value)

    def gram(n):
        for j, ref in enumerate((near_ref, own_ref, far_ref)):
            spot = slice(j * obs_tile, (j + 1) * obs_tile)
            block = ref[:, 0:mem_dev, :].reshape(members, obs_tile)
            mean = jnp.sum(block, axis=0, keepdims=True) * (1.0 / members)
            value = ref[0, mem_dev : mem_dev + 1, :]
            total = ref[0, mem_dev + 1 : mem_dev + 2, :] * wsum_ref[n : n + 1, spot]
            root = jnp.where(total > 0.0, jnp.sqrt(jnp.maximum(total, 1e-30)), 0.0)
            row = jnp.broadcast_to(root * (value - mean), (PAD, obs_tile))
            bh[n, 0:PAD, spot], bh[n, PAD:top, spot] = split(row)
            bh[n, top:, spot], bl[n, :, spot] = split((block - mean) * root)
        first = bh[n, 0 : top + HALF, :]
        second = bh[n, top + HALF :, :]
        left = mm_t(first, first[top:, :])
        right = mm_t(first, second)
        left_low = mm_t(first, bl[n, LO, :])
        right_low = mm_t(first, bl[n, HI, :])
        t[n, LO, LO] = 0.5 * left[top:] + left_low[top:]
        t[n, LO, HI] = right[top:] + right_low[top:]
        rhs0 = (left[0:1] + left[PAD : PAD + 1] + left_low[0:1]) * inv
        rhs1 = (right[0:1] + right[PAD : PAD + 1] + right_low[0:1]) * inv
        rhs_ref[n, :, LO] = jnp.broadcast_to(rhs0, (8, HALF))
        rhs_ref[n, :, HI] = jnp.broadcast_to(rhs1, (8, HALF))
        t[n, HI, LO] = mm_t(second, bl[n, LO, :])
        t[n, HI, HI] = 0.5 * mm_t(second, second) + mm_t(second, bl[n, HI, :])

    def start(n):
        g00 = (t[n, LO, LO] + t[n, LO, LO].T) * inv + eye
        g01 = (t[n, LO, HI] + t[n, HI, LO].T) * inv
        g11 = (t[n, HI, HI] + t[n, HI, HI].T) * inv + eye
        g10 = g01.T
        rows0 = jnp.sum(jnp.abs(g00), 0, keepdims=True) + jnp.sum(jnp.abs(g10), 0, keepdims=True)
        rows1 = jnp.sum(jnp.abs(g01), 0, keepdims=True) + jnp.sum(jnp.abs(g11), 0, keepdims=True)
        scale = jnp.max(jnp.maximum(rows0, rows1), axis=1, keepdims=True)
        shrink = 1.0 / scale
        for rows, cols, g in ((LO, LO, g00), (LO, HI, g01), (HI, LO, g10), (HI, HI, g11)):
            cur = g * shrink
            put(cur, p, ph, pl_, n, rows, cols)
            first = -0.5 * cur
            if rows == cols:
                first = first + 1.5 * eye
            put(first, z, zh, zl, n, rows, cols)
        return scale

    def square(n):
        t[n, LO, LO] = 0.5 * mm(ph[n, LO, :], ph[n, :, LO]) + mm(ph[n, LO, :], pl_[n, :, LO])
        t[n, HI, LO] = mm(ph[n, HI, :], ph[n, :, LO]) + mm(ph[n, HI, :], pl_[n, :, LO])
        t[n, LO, HI] = mm(ph[n, LO, :], pl_[n, :, HI])
        t[n, HI, HI] = 0.5 * mm(ph[n, HI, :], ph[n, :, HI]) + mm(ph[n, HI, :], pl_[n, :, HI])

    def squared(n, one_pass):
        g00 = t[n, LO, LO] + t[n, LO, LO].T
        g10 = t[n, HI, LO] + t[n, LO, HI].T
        g11 = t[n, HI, HI] + t[n, HI, HI].T
        for rows, cols, g in ((LO, LO, g00), (HI, LO, g10), (LO, HI, g10.T), (HI, HI, g11)):
            if one_pass:
                gh[n, rows, cols] = g.astype(BF)
            else:
                put(g, None, gh, gl, n, rows, cols)
        p[n, LO, LO] = 2.25 * p[n, LO, LO] - 1.5 * g00
        p[n, HI, LO] = 2.25 * p[n, HI, LO] - 1.5 * g10
        p[n, HI, HI] = 2.25 * p[n, HI, HI] - 1.5 * g11

    def product(n, high, low, rows, cols):
        return (
            mm(ph[n, rows, :], high[n, :, cols])
            + mm(pl_[n, rows, :], high[n, :, cols])
            + mm(ph[n, rows, :], low[n, :, cols])
        )

    def factor(n):
        z00 = 1.5 * z[n, LO, LO] - 0.5 * product(n, zh, zl, LO, LO)
        z10 = 1.5 * z[n, HI, LO] - 0.5 * product(n, zh, zl, HI, LO)
        z11 = 1.5 * z[n, HI, HI] - 0.5 * product(n, zh, zl, HI, HI)
        return z00, z10, z11

    def keep(n, parts):
        z00, z10, z11 = parts
        put(z00, z, zh, zl, n, LO, LO)
        put(z10, z, zh, zl, n, HI, LO)
        put(z10.T, None, zh, zl, n, LO, HI)
        put(z11, z, zh, zl, n, HI, HI)

    def cube(n, one_pass):
        def times(rows, cols):
            if one_pass:
                return mm(ph[n, rows, :], gh[n, :, cols])
            return product(n, gh, gl, rows, cols)

        n00 = p[n, LO, LO] + 0.25 * times(LO, LO)
        n10 = p[n, HI, LO] + 0.25 * times(HI, LO)
        n11 = p[n, HI, HI] + 0.25 * times(HI, HI)
        put(n00, p, ph, pl_, n, LO, LO)
        put(n10, p, ph, pl_, n, HI, LO)
        put(n10.T, None, ph, pl_, n, LO, HI)
        put(n11, p, ph, pl_, n, HI, HI)

    def sizes(n):
        p00, p10, p11 = p[n, LO, LO], p[n, HI, LO], p[n, HI, HI]
        total = jnp.sum(p00 * p00 + 2.0 * (p10 * p10) + p11 * p11) * (1.0 / members)
        trace = jnp.sum((p00 + p11) * eye) * (1.0 / members)
        return total, 1.0 - 2.0 * trace + total

    def widest():
        small, near = sizes(0)
        for n in range(1, patches):
            other_small, other_near = sizes(n)
            small, near = jnp.maximum(small, other_small), jnp.maximum(near, other_near)
        return small, near

    def near_one(n):
        e10 = -p[n, HI, LO]
        gh[n, LO, LO] = (eye - p[n, LO, LO]).astype(BF)
        gh[n, HI, LO] = e10.astype(BF)
        gh[n, LO, HI] = e10.T.astype(BF)
        gh[n, HI, HI] = (eye - p[n, HI, HI]).astype(BF)

    def near_factor(n):
        z00 = z[n, LO, LO] + 0.5 * mm(gh[n, LO, :], zh[n, :, LO])
        z10 = z[n, HI, LO] + 0.5 * mm(gh[n, HI, :], zh[n, :, LO])
        z11 = z[n, HI, HI] + 0.5 * mm(gh[n, HI, :], zh[n, :, HI])
        return z00, z10, z11

    def near_square(n):
        t[n, LO, LO] = mm(gh[n, LO, :], gh[n, :, LO])
        t[n, HI, LO] = mm(gh[n, HI, :], gh[n, :, LO])
        t[n, HI, HI] = mm(gh[n, HI, :], gh[n, :, HI])

    def near_squared(n):
        gl[n, LO, LO] = t[n, LO, LO].astype(BF)
        gl[n, HI, LO] = t[n, HI, LO].astype(BF)
        gl[n, LO, HI] = t[n, HI, LO].T.astype(BF)
        gl[n, HI, HI] = t[n, HI, HI].astype(BF)

    def near_cube(n):
        e00 = 0.75 * t[n, LO, LO] + 0.25 * mm(gh[n, LO, :], gl[n, :, LO])
        e10 = 0.75 * t[n, HI, LO] + 0.25 * mm(gh[n, HI, :], gl[n, :, LO])
        e11 = 0.75 * t[n, HI, HI] + 0.25 * mm(gh[n, HI, :], gl[n, :, HI])
        put(eye - e00, p, ph, pl_, n, LO, LO)
        put(-e10, p, ph, pl_, n, HI, LO)
        put(-e10.T, None, ph, pl_, n, LO, HI)
        put(eye - e11, p, ph, pl_, n, HI, HI)

    every = range(patches)
    for n in every:
        gram(n)
    scales = [start(n) for n in every]

    def sweep(first, one_pass):
        for n in every:
            square(n)
        for n in every:
            squared(n, one_pass)
            if not first:
                keep(n, factor(n))
            cube(n, one_pass)

    def near_sweep(one_pass):
        for n in every:
            near_one(n)
        for n in every:
            near_square(n)
        for n in every:
            near_squared(n)
            keep(n, near_factor(n) if one_pass else factor(n))
            near_cube(n)

    spread = jnp.max(jnp.concatenate(scales, 0))
    narrow = spread <= NARROW
    small, _ = widest()

    few = jnp.logical_and(small <= SMALL, narrow)

    @pl.when(jnp.logical_not(few))
    def _():
        sweep(True, False)

    @pl.when(few)
    def _():
        sweep(True, True)

    def step(_, carry):
        small, near = carry

        few = jnp.logical_and(small <= SMALL, narrow)
        rest = jnp.logical_not(few)

        @pl.when(few)
        def _():
            sweep(False, True)

        @pl.when(jnp.logical_and(rest, near > MID))
        def _():
            sweep(False, False)

        @pl.when(jnp.logical_and(rest, jnp.logical_and(near <= MID, near > LOW)))
        def _():
            near_sweep(False)

        @pl.when(jnp.logical_and(rest, near <= LOW))
        def _():
            near_sweep(True)

        return widest()

    _, near = lax.fori_loop(0, NS_ITERS - 2, step, widest())

    def finish(make):
        for n in every:
            z00, z10, z11 = make(n)
            out_ref[n, LO, LO] = z00 * lax.rsqrt(scales[n])
            out_ref[n, HI, LO] = z10 * lax.rsqrt(scales[n])
            out_ref[n, LO, HI] = z10.T * lax.rsqrt(scales[n])
            out_ref[n, HI, HI] = z11 * lax.rsqrt(scales[n])

    @pl.when(near > LOW)
    def _():
        finish(factor)

    @pl.when(near <= LOW)
    def _():
        for n in every:
            near_one(n)
        finish(near_factor)


def inverse_roots(near, own, far, wsum, members):
    patches, nobs = wsum.shape
    square = (patches, members, members)
    return pl.pallas_call(
        root_kernel,
        out_shape=(
            jax.ShapeDtypeStruct(square, F32),
            jax.ShapeDtypeStruct((patches, 8, members), F32),
        ),
        scratch_shapes=[
            pltpu.VMEM((patches, 2 * PAD + members, nobs), BF),
            pltpu.VMEM((patches, members, nobs), BF),
            pltpu.VMEM(square, F32),
            pltpu.VMEM(square, F32),
            pltpu.VMEM(square, BF),
            pltpu.VMEM(square, BF),
            pltpu.VMEM(square, BF),
            pltpu.VMEM(square, BF),
            pltpu.VMEM(square, F32),
            pltpu.VMEM(square, BF),
            pltpu.VMEM(square, BF),
        ],
        compiler_params=pltpu.CompilerParams(vmem_limit_bytes=28 * 1024 * 1024),
        cost_estimate=pl.CostEstimate(flops=25 * 10**9, bytes_accessed=4 * 10**6, transcendentals=0),
    )(near, own, far, wsum)


def apply_kernel(root_ref, rhs_ref, cols_ref, out_ref):
    devices, patches, levels, mem_dev, nlat = cols_ref.shape
    members = devices * mem_dev
    for n in range(patches):
        root = root_ref[n]
        high, low = split(root)
        weight = jnp.sum(root * rhs_ref[n, 0:1, :], axis=1, keepdims=True)
        cols = jnp.concatenate(
            [cols_ref[:, n, lev].reshape(members, nlat) for lev in range(levels)], 1
        )
        center = jnp.sum(cols, axis=0, keepdims=True) * (1.0 / members)
        cols_high, cols_low = split(cols - center)
        moved = mm(high, cols_high) + mm(low, cols_high) + mm(high, cols_low)
        result = moved + (center + jnp.sum(moved * weight, axis=0, keepdims=True))
        for lev in range(levels):
            part = result[:, lev * nlat : (lev + 1) * nlat]
            out_ref[:, n, lev] = part.reshape(devices, mem_dev, nlat)


def apply_roots(roots, rhs, cols):
    return pl.pallas_call(
        apply_kernel,
        out_shape=jax.ShapeDtypeStruct(cols.shape, F32),
        compiler_params=pltpu.CompilerParams(vmem_limit_bytes=24 * 1024 * 1024),
        cost_estimate=pl.CostEstimate(flops=8 * 10**8, bytes_accessed=4 * 10**6, transcendentals=0),
    )(roots, rhs, cols)


def advance(field, west, courant):
    nlat = field.shape[1]
    lat = lax.broadcasted_iota(jnp.int32, field.shape, 1)
    upper = jnp.where(lat == nlat - 1, field, pltpu.roll(field, nlat - 1, 1))
    lower = jnp.where(lat == 0, field, pltpu.roll(field, 1, 1))
    return field - courant * (field - west) + DIFFUSE * (upper + lower - 2.0 * field)


def picker(cells, nlat):
    spot = (lax.broadcasted_iota(jnp.int32, (nlat, cells.shape[1]), 0) == cells % nlat).astype(BF)
    twice = jnp.concatenate([spot, spot], 0)
    return lambda value: mm(jnp.concatenate(split(value), 1), twice)


def inner_kernel(
    field_hbm, courant_hbm, cell_hbm, value_hbm, rinv_hbm, out_ref, edge_ref, message_ref, extra_ref,
    field_ref, courant_ref, cell_ref, value_ref, rinv_ref, sems
):
    copies = [
        pltpu.make_async_copy(source, target, sems.at[i])
        for i, (source, target) in enumerate(
            (
                (field_hbm, field_ref),
                (courant_hbm, courant_ref),
                (cell_hbm, cell_ref),
                (value_hbm, value_ref),
                (rinv_hbm, rinv_ref),
            )
        )
    ]
    for copy in copies:
        copy.start()
    for copy in copies:
        copy.wait()
    lines, levels, members, nlat = out_ref.shape
    cells = cell_ref[...]
    pick = picker(cells, nlat)
    source_row = cells // nlat
    obs = jnp.zeros((members, cells.shape[1]), F32)
    for lev in range(levels):
        courant = courant_ref[lev : lev + 1, :]
        old, old_next = None, None
        for line in range(lines):
            now = field_ref[pl.ds(lev * lines + line, members, stride=levels * lines), :]
            if line < NSTEP:
                edge_ref[line, lev] = now
            now_next = None
            if line >= 1:
                now_next = advance(now, old, courant)
            if line >= NSTEP:
                done = advance(now_next, old_next, courant)
                out_ref[line, lev] = done
                obs = jnp.where(source_row == lev * lines + line, pick(done), obs)
            old, old_next = now, now_next
    message_ref[0:members, :] = obs
    message_ref[members : members + 1, :] = value_ref[...]
    message_ref[members + 1 : members + 2, :] = rinv_ref[...]
    message_ref[members + 2 :, :] = jnp.zeros((6, obs.shape[1]), F32)
    extra_ref[...] = jnp.zeros(extra_ref.shape, jnp.int32)
    extra_ref[0:1, :] = cells
    edge_ref[NSTEP] = jnp.zeros(edge_ref.shape[1:], F32)
    for lev in range(levels):
        edge_ref[NSTEP, lev, 0:1, :] = courant_ref[lev : lev + 1, :]


def inner_forecast(members, courant, cells, value, rinv):
    mem_dev, levels, lines, nlat = members.shape
    rows = mem_dev * levels * lines
    nobs = cells.shape[1]
    return pl.pallas_call(
        inner_kernel,
        out_shape=(
            jax.ShapeDtypeStruct((lines, levels, mem_dev, nlat), F32),
            jax.ShapeDtypeStruct((NSTEP + 1, levels, mem_dev, nlat), F32),
            jax.ShapeDtypeStruct((mem_dev + 8, nobs), F32),
            jax.ShapeDtypeStruct((8, nobs), jnp.int32),
        ),
        in_specs=[pl.BlockSpec(memory_space=pltpu.HBM)] * 5,
        scratch_shapes=[
            pltpu.VMEM((rows, nlat), F32),
            pltpu.VMEM(courant.shape, F32),
            pltpu.VMEM(cells.shape, jnp.int32),
            pltpu.VMEM(value.shape, F32),
            pltpu.VMEM(rinv.shape, F32),
            pltpu.SemaphoreType.DMA((5,)),
        ],
        compiler_params=pltpu.CompilerParams(vmem_limit_bytes=60 * 1024 * 1024),
        cost_estimate=pl.CostEstimate(flops=10**8, bytes_accessed=2 * 10**6, transcendentals=0),
    )(members.reshape(rows, nlat), courant, cells, value, rinv)


def edge_kernel(lines, halo_ref, edge_ref, cell_ref, partial_ref, field_ref, out_ref, message_ref):
    del field_ref
    _, levels, members, nlat = edge_ref.shape
    cells = cell_ref[0:1, :]
    pick = picker(cells, nlat)
    source_row = cells // nlat
    obs = partial_ref[0:members, :]
    for lev in range(levels):
        courant = edge_ref[NSTEP, lev, 0:1, :]
        old = halo_ref[1, lev]
        old_next = advance(old, halo_ref[0, lev], courant)
        for line in range(NSTEP):
            now = edge_ref[line, lev]
            now_next = advance(now, old, courant)
            done = advance(now_next, old_next, courant)
            out_ref[line, lev] = done
            obs = jnp.where(source_row == lev * lines + line, pick(done), obs)
            old, old_next = now, now_next
    message_ref[0:members, :] = obs
    message_ref[members:, :] = partial_ref[members:, :]


def edge_forecast(halo, edge, cells, partial, field):
    lines, levels, mem_dev, nlat = field.shape

    def whole(array):
        zeros = (0,) * array.ndim
        return pl.BlockSpec(array.shape, lambda i: zeros)

    first = pl.BlockSpec((NSTEP, levels, mem_dev, nlat), lambda i: (0, 0, 0, 0))
    small = (halo, edge, cells, partial)
    return pl.pallas_call(
        functools.partial(edge_kernel, lines),
        grid=(1,),
        out_shape=(
            jax.ShapeDtypeStruct(field.shape, F32),
            jax.ShapeDtypeStruct(partial.shape, F32),
        ),
        in_specs=[whole(a) for a in small] + [pl.BlockSpec(memory_space=pl.ANY)],
        out_specs=(first, whole(partial)),
        input_output_aliases={len(small): 0},
        compiler_params=pltpu.CompilerParams(vmem_limit_bytes=60 * 1024 * 1024),
        cost_estimate=pl.CostEstimate(flops=10**7, bytes_accessed=10**6, transcendentals=0),
    )(*small, field)


def restore_kernel(part_ref, out_ref):
    devices, patches, levels, mem_dev, nlat = part_ref.shape
    lines = patches * devices
    for device in range(devices):
        for n in range(patches):
            for lev in range(levels):
                rows = pl.ds(lev * lines + patches * device + n, mem_dev, stride=levels * lines)
                out_ref[rows, :] = part_ref[device, n, lev]


def restore(parts):
    devices, patches, levels, mem_dev, nlat = parts.shape
    rows = mem_dev * levels * patches * devices
    out = pl.pallas_call(
        restore_kernel,
        out_shape=jax.ShapeDtypeStruct((rows, nlat), F32),
        compiler_params=pltpu.CompilerParams(vmem_limit_bytes=24 * 1024 * 1024),
    )(parts)
    return out.reshape(mem_dev, levels, patches * devices, nlat)


def shifted(value, axis, steps):
    count = lax.axis_size(axis)
    pairs = [(source, (source + steps) % count) for source in range(count)]
    return lax.ppermute(value, axis, pairs)


def neighbours(value):
    mem, tile = lax.axis_size("mem"), lax.axis_size("tile")
    pairs = [
        (m * tile + t, m * tile + (t + (1 if m % 2 == 0 else -1)) % tile)
        for m in range(mem)
        for t in range(tile)
    ]
    near = lax.ppermute(value, ("mem", "tile"), pairs)
    far = lax.ppermute(near, "mem", [(m, m ^ 1) for m in range(mem)])
    return near, far


def on_device(
    members, courant, obs_cell, obs_value, obs_rinv, nbr_obs, nbr_class, nbr_count, loc_table
):
    mem_dev, levels, lines, nlat = members.shape
    devices = lax.axis_size("mem")
    obs_tile = obs_cell.shape[0]
    slots = nbr_obs.shape[1]
    edge = jnp.transpose(members[:, :, lines - NSTEP :, :], (2, 1, 0, 3))
    halo = shifted(edge, "tile", 1)
    field, first_lines, partial, cells = inner_forecast(
        members, courant, obs_cell[None], obs_value[None], obs_rinv[None]
    )
    field, message = edge_forecast(halo, first_lines, cells, partial, field)
    own = lax.all_gather(message, "mem", axis=0, tiled=True)
    own, nbr_obs, nbr_class, nbr_count, loc_table, field = lax.optimization_barrier(
        (own, nbr_obs, nbr_class, nbr_count, loc_table, field)
    )
    near, far = neighbours(own)
    columns = lax.all_to_all(
        field.reshape(devices, lines // devices, levels, mem_dev, nlat), "mem", 0, 0, tiled=True
    )
    tile_index = lax.axis_index("tile")
    tile_count = lax.axis_size("tile")
    offset = (nbr_obs // obs_tile - tile_index + 1) % tile_count
    offset = jnp.where(lax.axis_index("mem") % 2 == 0, offset, 2 - offset)
    local_ids = offset * obs_tile + nbr_obs % obs_tile
    classes = jnp.arange(loc_table.shape[0])
    local_w = jnp.sum(jnp.where(nbr_class[..., None] == classes, loc_table, 0.0), -1)
    local_w = jnp.where(jnp.arange(slots) < nbr_count[:, None], local_w, 0.0)
    places = jnp.arange(3 * obs_tile)
    wsum = jnp.sum(jnp.where(local_ids[:, :, None] == places, local_w[:, :, None], 0.0), 1)

    shape = (devices, mem_dev + 8, obs_tile)
    roots, rhs = inverse_roots(
        near.reshape(shape), own.reshape(shape), far.reshape(shape), wsum, devices * mem_dev
    )
    parts = apply_roots(roots, rhs, columns)
    return restore(lax.all_to_all(parts, "mem", 0, 0, tiled=True))


def solution(mesh):
    return jax.shard_map(
        on_device,
        mesh=mesh,
        in_specs=(
            P("mem", None, "tile", None),
            P(),
            P("tile"),
            P("tile"),
            P("tile"),
            P(("tile", "mem"), None),
            P(("tile", "mem"), None),
            P(("tile", "mem")),
            P(),
        ),
        out_specs=P("mem", None, "tile", None),
        check_vma=False,
    )
```

```python
import functools
import jax
import jax.numpy as jnp
from jax import lax
from jax.experimental import pallas as pl
from jax.experimental.pallas import tpu as pltpu
from jax.sharding import PartitionSpec as P

NSTEP = 2
NS_ITERS = 8
DIFFUSE = 0.1
HALF = 256
PAD = 16
NARROW = 32.0
SMALL = (1.0 / 5, 1.0 / 16, 1.0 / 64)
MID, LOW = 1.0 / 4, 1.0 / 32
BF = jnp.bfloat16
F32 = jnp.float32
LO, HI = slice(0, HALF), slice(HALF, 2 * HALF)


def split(value):
    high = value.astype(BF)
    return high, (value - high.astype(F32)).astype(BF)


def mm(left, right):
    return jnp.dot(left, right, preferred_element_type=F32)


def mm_t(left, right):
    return lax.dot_general(left, right, (((1,), (1,)), ((), ())), preferred_element_type=F32)


def add_part(n, spot, block_ref, wsum_ref, bh, bl, old, old_rhs, new, new_rhs):
    devices, rows, obs_tile = block_ref.shape
    members = bl.shape[1]
    mem_dev = members // devices
    top = 2 * PAD
    block = block_ref[:, 0:mem_dev, :].reshape(members, obs_tile)
    mean = jnp.sum(block, axis=0, keepdims=True) * (1.0 / members)
    value = block_ref[0, mem_dev : mem_dev + 1, :]
    total = block_ref[0, mem_dev + 1 : mem_dev + 2, :] * wsum_ref[n : n + 1, spot]
    root = jnp.where(total > 0.0, jnp.sqrt(jnp.maximum(total, 1e-30)), 0.0)
    row = jnp.broadcast_to(root * (value - mean), (PAD, obs_tile))
    bh[n, 0:PAD, :], bh[n, PAD:top, :] = split(row)
    bh[n, top:, :], bl[n] = split((block - mean) * root)
    first = bh[n, 0 : top + HALF, :]
    second = bh[n, top + HALF :, :]
    left = mm_t(first, first[top:, :])
    right = mm_t(first, second)
    left_low = mm_t(first, bl[n, LO, :])
    right_low = mm_t(first, bl[n, HI, :])
    sums = {
        (0, 0): 0.5 * left[top:] + left_low[top:],
        (0, 1): right[top:] + right_low[top:],
        (1, 0): mm_t(second, bl[n, LO, :]),
        (1, 1): 0.5 * mm_t(second, second) + mm_t(second, bl[n, HI, :]),
    }
    for (a, b), value in sums.items():
        spot_a, spot_b = (LO, HI)[a], (LO, HI)[b]
        new[n, spot_a, spot_b] = value if old is None else value + old[n, spot_a, spot_b]
    for spot_b, high, low in ((LO, left, left_low), (HI, right, right_low)):
        rhs = jnp.broadcast_to(high[0:1] + high[PAD : PAD + 1] + low[0:1], (8, HALF))
        new_rhs[n, :, spot_b] = rhs if old_rhs is None else rhs + old_rhs[n, :, spot_b]


def part_kernel(spot, block_ref, wsum_ref, *refs):
    old, old_rhs = refs[:-4] if len(refs) == 6 else (None, None)
    new, new_rhs, bh, bl = refs[-4:]
    for n in range(new.shape[0]):
        add_part(n, spot, block_ref, wsum_ref, bh, bl, old, old_rhs, new, new_rhs)


def gram_part(which, block, wsum, members, sofar=()):
    patches, obs_tile = wsum.shape[0], block.shape[2]
    spot = slice(which * obs_tile, (which + 1) * obs_tile)
    return pl.pallas_call(
        functools.partial(part_kernel, spot),
        out_shape=(
            jax.ShapeDtypeStruct((patches, members, members), F32),
            jax.ShapeDtypeStruct((patches, 8, members), F32),
        ),
        scratch_shapes=[
            pltpu.VMEM((patches, 2 * PAD + members, obs_tile), BF),
            pltpu.VMEM((patches, members, obs_tile), BF),
        ],
        compiler_params=pltpu.CompilerParams(vmem_limit_bytes=24 * 1024 * 1024),
        cost_estimate=pl.CostEstimate(flops=2 * 10**9, bytes_accessed=4 * 10**6, transcendentals=0),
    )(block, wsum, *sofar)


def root_kernel(
    far_ref, wsum_ref, gram_ref, part_ref, out_ref, rhs_ref, bh, bl, t, p, ph, pl_, gh, gl, z, zh, zl
):
    devices, _, obs_tile = far_ref.shape
    patches, members = out_ref.shape[:2]
    inv = 1.0 / (members - 1)
    eye = (
        lax.broadcasted_iota(jnp.int32, (HALF, HALF), 0)
        == lax.broadcasted_iota(jnp.int32, (HALF, HALF), 1)
    ).astype(F32)

    def put(value, full, high, low, n, rows, cols):
        if full is not None:
            full[n, rows, cols] = value
        high[n, rows, cols], low[n, rows, cols] = split(value)

    def gram(n):
        spot = slice(2 * obs_tile, 3 * obs_tile)
        add_part(n, spot, far_ref, wsum_ref, bh, bl, gram_ref, part_ref, t, rhs_ref)
        rhs_ref[n] = rhs_ref[n] * inv

    def start(n):
        g00 = (t[n, LO, LO] + t[n, LO, LO].T) * inv + eye
        g01 = (t[n, LO, HI] + t[n, HI, LO].T) * inv
        g11 = (t[n, HI, HI] + t[n, HI, HI].T) * inv + eye
        g10 = g01.T
        rows0 = jnp.sum(jnp.abs(g00), 0, keepdims=True) + jnp.sum(jnp.abs(g10), 0, keepdims=True)
        rows1 = jnp.sum(jnp.abs(g01), 0, keepdims=True) + jnp.sum(jnp.abs(g11), 0, keepdims=True)
        scale = jnp.max(jnp.maximum(rows0, rows1), axis=1, keepdims=True)
        shrink = 1.0 / scale
        for rows, cols, g in ((LO, LO, g00), (LO, HI, g01), (HI, LO, g10), (HI, HI, g11)):
            cur = g * shrink
            put(cur, p, ph, pl_, n, rows, cols)
            first = -0.5 * cur
            if rows == cols:
                first = first + 1.5 * eye
            put(first, z, zh, zl, n, rows, cols)
        return scale

    def square(n):
        t[n, LO, LO] = 0.5 * mm(ph[n, LO, :], ph[n, :, LO]) + mm(ph[n, LO, :], pl_[n, :, LO])
        t[n, HI, LO] = mm(ph[n, HI, :], ph[n, :, LO]) + mm(ph[n, HI, :], pl_[n, :, LO])
        t[n, LO, HI] = mm(ph[n, LO, :], pl_[n, :, HI])
        t[n, HI, HI] = 0.5 * mm(ph[n, HI, :], ph[n, :, HI]) + mm(ph[n, HI, :], pl_[n, :, HI])

    def squared(n, one_pass):
        g00 = t[n, LO, LO] + t[n, LO, LO].T
        g10 = t[n, HI, LO] + t[n, LO, HI].T
        g11 = t[n, HI, HI] + t[n, HI, HI].T
        for rows, cols, g in ((LO, LO, g00), (HI, LO, g10), (LO, HI, g10.T), (HI, HI, g11)):
            if one_pass:
                gh[n, rows, cols] = g.astype(BF)
            else:
                put(g, None, gh, gl, n, rows, cols)
        p[n, LO, LO] = 2.25 * p[n, LO, LO] - 1.5 * g00
        p[n, HI, LO] = 2.25 * p[n, HI, LO] - 1.5 * g10
        p[n, HI, HI] = 2.25 * p[n, HI, HI] - 1.5 * g11

    def product(n, high, low, rows, cols):
        return (
            mm(ph[n, rows, :], high[n, :, cols])
            + mm(pl_[n, rows, :], high[n, :, cols])
            + mm(ph[n, rows, :], low[n, :, cols])
        )

    def factor(n):
        z00 = 1.5 * z[n, LO, LO] - 0.5 * product(n, zh, zl, LO, LO)
        z10 = 1.5 * z[n, HI, LO] - 0.5 * product(n, zh, zl, HI, LO)
        z11 = 1.5 * z[n, HI, HI] - 0.5 * product(n, zh, zl, HI, HI)
        return z00, z10, z11

    def few_factor(n, lead):
        gl[n, LO, LO] = (z[n, LO, LO] - lead * eye).astype(BF)
        gl[n, HI, LO] = z[n, HI, LO].astype(BF)
        gl[n, LO, HI] = z[n, HI, LO].T.astype(BF)
        gl[n, HI, HI] = (z[n, HI, HI] - lead * eye).astype(BF)

        def moved(rows, cols):
            part = lead * p[n, rows, cols] + mm(ph[n, rows, :], gl[n, :, cols])
            return 1.5 * z[n, rows, cols] - 0.5 * part

        return moved(LO, LO), moved(HI, LO), moved(HI, HI)

    def keep(n, parts):
        z00, z10, z11 = parts
        put(z00, z, zh, zl, n, LO, LO)
        put(z10, z, zh, zl, n, HI, LO)
        put(z10.T, None, zh, zl, n, LO, HI)
        put(z11, z, zh, zl, n, HI, HI)

    def cube(n, one_pass):
        def times(rows, cols):
            if one_pass:
                return mm(ph[n, rows, :], gh[n, :, cols])
            return product(n, gh, gl, rows, cols)

        n00 = p[n, LO, LO] + 0.25 * times(LO, LO)
        n10 = p[n, HI, LO] + 0.25 * times(HI, LO)
        n11 = p[n, HI, HI] + 0.25 * times(HI, HI)
        put(n00, p, ph, pl_, n, LO, LO)
        put(n10, p, ph, pl_, n, HI, LO)
        put(n10.T, None, ph, pl_, n, LO, HI)
        put(n11, p, ph, pl_, n, HI, HI)

    def mean_square(n):
        p00, p10, p11 = p[n, LO, LO], p[n, HI, LO], p[n, HI, HI]
        return jnp.sum(p00 * p00 + 2.0 * (p10 * p10) + p11 * p11) * (1.0 / members)

    def near_one(n):
        e10 = -p[n, HI, LO]
        gh[n, LO, LO] = (eye - p[n, LO, LO]).astype(BF)
        gh[n, HI, LO] = e10.astype(BF)
        gh[n, LO, HI] = e10.T.astype(BF)
        gh[n, HI, HI] = (eye - p[n, HI, HI]).astype(BF)

    def near_factor(n):
        z00 = z[n, LO, LO] + 0.5 * mm(gh[n, LO, :], zh[n, :, LO])
        z10 = z[n, HI, LO] + 0.5 * mm(gh[n, HI, :], zh[n, :, LO])
        z11 = z[n, HI, HI] + 0.5 * mm(gh[n, HI, :], zh[n, :, HI])
        return z00, z10, z11

    def near_square(n):
        t[n, LO, LO] = mm(gh[n, LO, :], gh[n, :, LO])
        t[n, HI, LO] = mm(gh[n, HI, :], gh[n, :, LO])
        t[n, HI, HI] = mm(gh[n, HI, :], gh[n, :, HI])

    def near_squared(n):
        gl[n, LO, LO] = t[n, LO, LO].astype(BF)
        gl[n, HI, LO] = t[n, HI, LO].astype(BF)
        gl[n, LO, HI] = t[n, HI, LO].T.astype(BF)
        gl[n, HI, HI] = t[n, HI, HI].astype(BF)

    def near_cube(n):
        e00 = 0.75 * t[n, LO, LO] + 0.25 * mm(gh[n, LO, :], gl[n, :, LO])
        e10 = 0.75 * t[n, HI, LO] + 0.25 * mm(gh[n, HI, :], gl[n, :, LO])
        e11 = 0.75 * t[n, HI, HI] + 0.25 * mm(gh[n, HI, :], gl[n, :, HI])
        put(eye - e00, p, ph, pl_, n, LO, LO)
        put(-e10, p, ph, pl_, n, HI, LO)
        put(-e10.T, None, ph, pl_, n, LO, HI)
        put(eye - e11, p, ph, pl_, n, HI, HI)

    every = range(patches)
    for n in every:
        gram(n)
    scales = [start(n) for n in every]

    def sweep(lead, one_pass):
        for n in every:
            square(n)
        for n in every:
            if one_pass and lead is not None:
                keep(n, few_factor(n, lead))
            squared(n, one_pass)
            if not one_pass and lead is not None:
                keep(n, factor(n))
            cube(n, one_pass)

    def near_sweep(one_pass):
        for n in every:
            near_one(n)
        for n in every:
            near_square(n)
        for n in every:
            near_squared(n)
            keep(n, near_factor(n) if one_pass else factor(n))
            near_cube(n)

    least = jnp.min(1.0 / jnp.concatenate(scales, 0))
    mean = mean_square(0)
    for n in range(1, patches):
        mean = jnp.maximum(mean, mean_square(n))
    count = sum((mean <= bound).astype(jnp.int32) for bound in SMALL)
    count = jnp.where(least >= 1.0 / NARROW, count, 0)

    def onward(value):
        return 0.25 * value * (3.0 - value) * (3.0 - value)

    @pl.when(count == 0)
    def _():
        sweep(None, False)

    @pl.when(count > 0)
    def _():
        sweep(None, True)

    def step(k, carry):
        least, lead = carry
        few = k < count
        rest = jnp.logical_not(few)
        wide = 1.0 - least

        @pl.when(few)
        def _():
            sweep(lead, True)

        @pl.when(jnp.logical_and(rest, wide > MID))
        def _():
            sweep(lead, False)

        @pl.when(jnp.logical_and(rest, jnp.logical_and(wide <= MID, wide > LOW)))
        def _():
            near_sweep(False)

        @pl.when(jnp.logical_and(rest, wide <= LOW))
        def _():
            near_sweep(True)

        return onward(least), 1.5 * lead

    least, _ = lax.fori_loop(1, NS_ITERS - 1, step, (onward(least), jnp.float32(1.5)))

    def finish(make):
        for n in every:
            z00, z10, z11 = make(n)
            out_ref[n, LO, LO] = z00 * lax.rsqrt(scales[n])
            out_ref[n, HI, LO] = z10 * lax.rsqrt(scales[n])
            out_ref[n, LO, HI] = z10.T * lax.rsqrt(scales[n])
            out_ref[n, HI, HI] = z11 * lax.rsqrt(scales[n])

    @pl.when(1.0 - least > LOW)
    def _():
        finish(factor)

    @pl.when(1.0 - least <= LOW)
    def _():
        for n in every:
            near_one(n)
        finish(near_factor)


def inverse_roots(near, own, far, wsum, members):
    sofar = gram_part(1, own, wsum, members)
    sofar = gram_part(0, near, wsum, members, sofar)
    patches, obs_tile = wsum.shape[0], far.shape[2]
    square = (patches, members, members)
    return pl.pallas_call(
        root_kernel,
        out_shape=(
            jax.ShapeDtypeStruct(square, F32),
            jax.ShapeDtypeStruct((patches, 8, members), F32),
        ),
        scratch_shapes=[
            pltpu.VMEM((patches, 2 * PAD + members, obs_tile), BF),
            pltpu.VMEM((patches, members, obs_tile), BF),
            pltpu.VMEM(square, F32),
            pltpu.VMEM(square, F32),
            pltpu.VMEM(square, BF),
            pltpu.VMEM(square, BF),
            pltpu.VMEM(square, BF),
            pltpu.VMEM(square, BF),
            pltpu.VMEM(square, F32),
            pltpu.VMEM(square, BF),
            pltpu.VMEM(square, BF),
        ],
        compiler_params=pltpu.CompilerParams(vmem_limit_bytes=28 * 1024 * 1024),
        cost_estimate=pl.CostEstimate(flops=25 * 10**9, bytes_accessed=4 * 10**6, transcendentals=0),
    )(far, wsum, *sofar)


def apply_kernel(root_ref, rhs_ref, cols_ref, out_ref):
    devices, patches, levels, mem_dev, nlat = cols_ref.shape
    members = devices * mem_dev
    for n in range(patches):
        root = root_ref[n]
        high, low = split(root)
        weight = jnp.sum(root * rhs_ref[n, 0:1, :], axis=1, keepdims=True)
        cols = jnp.concatenate(
            [cols_ref[:, n, lev].reshape(members, nlat) for lev in range(levels)], 1
        )
        center = jnp.sum(cols, axis=0, keepdims=True) * (1.0 / members)
        cols_high, cols_low = split(cols - center)
        moved = mm(high, cols_high) + mm(low, cols_high) + mm(high, cols_low)
        result = moved + (center + jnp.sum(moved * weight, axis=0, keepdims=True))
        for lev in range(levels):
            part = result[:, lev * nlat : (lev + 1) * nlat]
            out_ref[:, n, lev] = part.reshape(devices, mem_dev, nlat)


def apply_roots(roots, rhs, cols):
    return pl.pallas_call(
        apply_kernel,
        out_shape=jax.ShapeDtypeStruct(cols.shape, F32),
        compiler_params=pltpu.CompilerParams(vmem_limit_bytes=24 * 1024 * 1024),
        cost_estimate=pl.CostEstimate(flops=8 * 10**8, bytes_accessed=4 * 10**6, transcendentals=0),
    )(roots, rhs, cols)


def advance(field, west, courant):
    nlat = field.shape[1]
    lat = lax.broadcasted_iota(jnp.int32, field.shape, 1)
    upper = jnp.where(lat == nlat - 1, field, pltpu.roll(field, nlat - 1, 1))
    lower = jnp.where(lat == 0, field, pltpu.roll(field, 1, 1))
    return field - courant * (field - west) + DIFFUSE * (upper + lower - 2.0 * field)


def picker(cells, nlat):
    spot = (lax.broadcasted_iota(jnp.int32, (nlat, cells.shape[1]), 0) == cells % nlat).astype(BF)
    twice = jnp.concatenate([spot, spot], 0)
    return lambda value: mm(jnp.concatenate(split(value), 1), twice)


def inner_kernel(
    field_hbm, courant_hbm, cell_hbm, value_hbm, rinv_hbm, out_ref, edge_ref, message_ref, extra_ref,
    field_ref, courant_ref, cell_ref, value_ref, rinv_ref, sems
):
    copies = [
        pltpu.make_async_copy(source, target, sems.at[i])
        for i, (source, target) in enumerate(
            (
                (field_hbm, field_ref),
                (courant_hbm, courant_ref),
                (cell_hbm, cell_ref),
                (value_hbm, value_ref),
                (rinv_hbm, rinv_ref),
            )
        )
    ]
    for copy in copies:
        copy.start()
    for copy in copies:
        copy.wait()
    lines, levels, members, nlat = out_ref.shape
    cells = cell_ref[...]
    pick = picker(cells, nlat)
    source_row = cells // nlat
    obs = jnp.zeros((members, cells.shape[1]), F32)
    for lev in range(levels):
        courant = courant_ref[lev : lev + 1, :]
        old, old_next = None, None
        for line in range(lines):
            now = field_ref[pl.ds(lev * lines + line, members, stride=levels * lines), :]
            if line < NSTEP:
                edge_ref[line, lev] = now
            now_next = None
            if line >= 1:
                now_next = advance(now, old, courant)
            if line >= NSTEP:
                done = advance(now_next, old_next, courant)
                out_ref[line, lev] = done
                obs = jnp.where(source_row == lev * lines + line, pick(done), obs)
            old, old_next = now, now_next
    message_ref[0:members, :] = obs
    message_ref[members : members + 1, :] = value_ref[...]
    message_ref[members + 1 : members + 2, :] = rinv_ref[...]
    message_ref[members + 2 :, :] = jnp.zeros((6, obs.shape[1]), F32)
    extra_ref[...] = jnp.zeros(extra_ref.shape, jnp.int32)
    extra_ref[0:1, :] = cells
    edge_ref[NSTEP] = jnp.zeros(edge_ref.shape[1:], F32)
    for lev in range(levels):
        edge_ref[NSTEP, lev, 0:1, :] = courant_ref[lev : lev + 1, :]


def inner_forecast(members, courant, cells, value, rinv):
    mem_dev, levels, lines, nlat = members.shape
    rows = mem_dev * levels * lines
    nobs = cells.shape[1]
    return pl.pallas_call(
        inner_kernel,
        out_shape=(
            jax.ShapeDtypeStruct((lines, levels, mem_dev, nlat), F32),
            jax.ShapeDtypeStruct((NSTEP + 1, levels, mem_dev, nlat), F32),
            jax.ShapeDtypeStruct((mem_dev + 8, nobs), F32),
            jax.ShapeDtypeStruct((8, nobs), jnp.int32),
        ),
        in_specs=[pl.BlockSpec(memory_space=pltpu.HBM)] * 5,
        scratch_shapes=[
            pltpu.VMEM((rows, nlat), F32),
            pltpu.VMEM(courant.shape, F32),
            pltpu.VMEM(cells.shape, jnp.int32),
            pltpu.VMEM(value.shape, F32),
            pltpu.VMEM(rinv.shape, F32),
            pltpu.SemaphoreType.DMA((5,)),
        ],
        compiler_params=pltpu.CompilerParams(vmem_limit_bytes=60 * 1024 * 1024),
        cost_estimate=pl.CostEstimate(flops=10**8, bytes_accessed=2 * 10**6, transcendentals=0),
    )(members.reshape(rows, nlat), courant, cells, value, rinv)


def edge_kernel(lines, halo_ref, edge_ref, cell_ref, partial_ref, field_ref, out_ref, message_ref):
    del field_ref
    _, levels, members, nlat = edge_ref.shape
    cells = cell_ref[0:1, :]
    pick = picker(cells, nlat)
    source_row = cells // nlat
    obs = partial_ref[0:members, :]
    for lev in range(levels):
        courant = edge_ref[NSTEP, lev, 0:1, :]
        old = halo_ref[1, lev]
        old_next = advance(old, halo_ref[0, lev], courant)
        for line in range(NSTEP):
            now = edge_ref[line, lev]
            now_next = advance(now, old, courant)
            done = advance(now_next, old_next, courant)
            out_ref[line, lev] = done
            obs = jnp.where(source_row == lev * lines + line, pick(done), obs)
            old, old_next = now, now_next
    message_ref[0:members, :] = obs
    message_ref[members:, :] = partial_ref[members:, :]


def edge_forecast(halo, edge, cells, partial, field):
    lines, levels, mem_dev, nlat = field.shape

    def whole(array):
        zeros = (0,) * array.ndim
        return pl.BlockSpec(array.shape, lambda i: zeros)

    first = pl.BlockSpec((NSTEP, levels, mem_dev, nlat), lambda i: (0, 0, 0, 0))
    small = (halo, edge, cells, partial)
    return pl.pallas_call(
        functools.partial(edge_kernel, lines),
        grid=(1,),
        out_shape=(
            jax.ShapeDtypeStruct(field.shape, F32),
            jax.ShapeDtypeStruct(partial.shape, F32),
        ),
        in_specs=[whole(a) for a in small] + [pl.BlockSpec(memory_space=pl.ANY)],
        out_specs=(first, whole(partial)),
        input_output_aliases={len(small): 0},
        compiler_params=pltpu.CompilerParams(vmem_limit_bytes=60 * 1024 * 1024),
        cost_estimate=pl.CostEstimate(flops=10**7, bytes_accessed=10**6, transcendentals=0),
    )(*small, field)


def restore_kernel(part_ref, out_hbm, out_ref, sems):
    devices, patches, levels, mem_dev, nlat = part_ref.shape
    lines = patches * devices
    group = 8
    copies = []
    for i in range(mem_dev // group):
        for device in range(devices):
            for n in range(patches):
                for lev in range(levels):
                    first = i * group * levels * lines + lev * lines + patches * device + n
                    rows = pl.ds(first, group, stride=levels * lines)
                    out_ref[rows, :] = part_ref[device, n, lev, i * group : (i + 1) * group, :]
        spot = pl.ds(i * group * levels * lines, group * levels * lines)
        copies.append(pltpu.make_async_copy(out_ref.at[spot], out_hbm.at[spot], sems.at[i]))
        copies[-1].start()
    for copy in copies:
        copy.wait()


def restore(parts):
    devices, patches, levels, mem_dev, nlat = parts.shape
    rows = mem_dev * levels * patches * devices
    out = pl.pallas_call(
        restore_kernel,
        out_shape=jax.ShapeDtypeStruct((rows, nlat), F32),
        in_specs=[pl.BlockSpec(memory_space=pltpu.VMEM)],
        out_specs=pl.BlockSpec(memory_space=pl.ANY),
        scratch_shapes=[
            pltpu.VMEM((rows, nlat), F32),
            pltpu.SemaphoreType.DMA((mem_dev // 8,)),
        ],
        compiler_params=pltpu.CompilerParams(vmem_limit_bytes=24 * 1024 * 1024),
    )(parts)
    return out.reshape(mem_dev, levels, patches * devices, nlat)


def shifted(value, axis, steps):
    count = lax.axis_size(axis)
    pairs = [(source, (source + steps) % count) for source in range(count)]
    return lax.ppermute(value, axis, pairs)


def neighbours(value):
    mem, tile = lax.axis_size("mem"), lax.axis_size("tile")
    pairs = [
        (m * tile + t, m * tile + (t + (1 if m % 2 == 0 else -1)) % tile)
        for m in range(mem)
        for t in range(tile)
    ]
    near = lax.ppermute(value, ("mem", "tile"), pairs)
    far = lax.ppermute(near, "mem", [(m, m ^ 1) for m in range(mem)])
    return near, far


def on_device(
    members, courant, obs_cell, obs_value, obs_rinv, nbr_obs, nbr_class, nbr_count, loc_table
):
    mem_dev, levels, lines, nlat = members.shape
    devices = lax.axis_size("mem")
    obs_tile = obs_cell.shape[0]
    slots = nbr_obs.shape[1]
    edge = jnp.transpose(members[:, :, lines - NSTEP :, :], (2, 1, 0, 3))
    halo = shifted(edge, "tile", 1)
    field, first_lines, partial, cells = inner_forecast(
        members, courant, obs_cell[None], obs_value[None], obs_rinv[None]
    )
    field, message = edge_forecast(halo, first_lines, cells, partial, field)
    own = lax.all_gather(message, "mem", axis=0, tiled=True)
    own, nbr_obs, nbr_class, nbr_count, loc_table, field = lax.optimization_barrier(
        (own, nbr_obs, nbr_class, nbr_count, loc_table, field)
    )
    near, far = neighbours(own)
    columns = lax.all_to_all(
        field.reshape(devices, lines // devices, levels, mem_dev, nlat), "mem", 0, 0, tiled=True
    )
    tile_index = lax.axis_index("tile")
    tile_count = lax.axis_size("tile")
    offset = (nbr_obs // obs_tile - tile_index + 1) % tile_count
    offset = jnp.where(lax.axis_index("mem") % 2 == 0, offset, 2 - offset)
    local_ids = offset * obs_tile + nbr_obs % obs_tile
    classes = jnp.arange(loc_table.shape[0])
    local_w = jnp.sum(jnp.where(nbr_class[..., None] == classes, loc_table, 0.0), -1)
    local_w = jnp.where(jnp.arange(slots) < nbr_count[:, None], local_w, 0.0)
    places = jnp.arange(3 * obs_tile)
    wsum = jnp.sum(jnp.where(local_ids[:, :, None] == places, local_w[:, :, None], 0.0), 1)

    shape = (devices, mem_dev + 8, obs_tile)
    roots, rhs = inverse_roots(
        near.reshape(shape), own.reshape(shape), far.reshape(shape), wsum, devices * mem_dev
    )
    parts = apply_roots(roots, rhs, columns)
    return restore(lax.all_to_all(parts, "mem", 0, 0, tiled=True))


def solution(mesh):
    return jax.shard_map(
        on_device,
        mesh=mesh,
        in_specs=(
            P("mem", None, "tile", None),
            P(),
            P("tile"),
            P("tile"),
            P("tile"),
            P(("tile", "mem"), None),
            P(("tile", "mem"), None),
            P(("tile", "mem")),
            P(),
        ),
        out_specs=P("mem", None, "tile", None),
        check_vma=False,
    )
```

```python
import functools
import jax
import jax.numpy as jnp
from jax import lax
from jax.experimental import pallas as pl
from jax.experimental.pallas import tpu as pltpu
from jax.sharding import PartitionSpec as P

NSTEP = 2
NS_ITERS = 8
DIFFUSE = 0.1
HALF = 256
PAD = 16
NARROW = 32.0
SMALL = (1.0 / 5, 1.0 / 16, 1.0 / 64)
MID, LOW = 1.0 / 4, 1.0 / 32
BF = jnp.bfloat16
F32 = jnp.float32
LO, HI = slice(0, HALF), slice(HALF, 2 * HALF)


def split(value):
    high = value.astype(BF)
    return high, (value - high.astype(F32)).astype(BF)


def mm(left, right):
    return jnp.dot(left, right, preferred_element_type=F32)


def mm_t(left, right):
    return lax.dot_general(left, right, (((1,), (1,)), ((), ())), preferred_element_type=F32)


def add_part(n, spot, block_ref, wsum_ref, bh, bl, old, old_rhs, new, new_rhs):
    members, obs_tile = block_ref.shape
    top = 2 * PAD
    block = block_ref[...]
    mean = jnp.sum(block, axis=0, keepdims=True) * (1.0 / members)
    total = wsum_ref[n : n + 1, spot]
    root = jnp.where(total > 0.0, jnp.sqrt(jnp.maximum(total, 1e-30)), 0.0)
    row = jnp.broadcast_to(-root * mean, (PAD, obs_tile))
    bh[n, 0:PAD, :], bh[n, PAD:top, :] = split(row)
    bh[n, top:, :], bl[n] = split((block - mean) * root)
    first = bh[n, 0 : top + HALF, :]
    second = bh[n, top + HALF :, :]
    left = mm_t(first, first[top:, :])
    right = mm_t(first, second)
    left_low = mm_t(first, bl[n, LO, :])
    right_low = mm_t(first, bl[n, HI, :])
    sums = {
        (0, 0): 0.5 * left[top:] + left_low[top:],
        (0, 1): right[top:] + right_low[top:],
        (1, 0): mm_t(second, bl[n, LO, :]),
        (1, 1): 0.5 * mm_t(second, second) + mm_t(second, bl[n, HI, :]),
    }
    for (a, b), value in sums.items():
        spot_a, spot_b = (LO, HI)[a], (LO, HI)[b]
        new[n, spot_a, spot_b] = value if old is None else value + old[n, spot_a, spot_b]
    for spot_b, high, low in ((LO, left, left_low), (HI, right, right_low)):
        rhs = jnp.broadcast_to(high[0:1] + high[PAD : PAD + 1] + low[0:1], (8, HALF))
        new_rhs[n, :, spot_b] = rhs if old_rhs is None else rhs + old_rhs[n, :, spot_b]


def part_kernel(spot, block_ref, wsum_ref, *refs):
    old, old_rhs = refs[:-4] if len(refs) == 6 else (None, None)
    new, new_rhs, bh, bl = refs[-4:]
    for n in range(new.shape[0]):
        add_part(n, spot, block_ref, wsum_ref, bh, bl, old, old_rhs, new, new_rhs)


def gram_part(which, block, wsum, members, sofar=()):
    patches, obs_tile = wsum.shape[0], block.shape[1]
    spot = slice(which * obs_tile, (which + 1) * obs_tile)
    return pl.pallas_call(
        functools.partial(part_kernel, spot),
        out_shape=(
            jax.ShapeDtypeStruct((patches, members, members), F32),
            jax.ShapeDtypeStruct((patches, 8, members), F32),
        ),
        scratch_shapes=[
            pltpu.VMEM((patches, 2 * PAD + members, obs_tile), BF),
            pltpu.VMEM((patches, members, obs_tile), BF),
        ],
        compiler_params=pltpu.CompilerParams(vmem_limit_bytes=24 * 1024 * 1024),
        cost_estimate=pl.CostEstimate(flops=2 * 10**9, bytes_accessed=4 * 10**6, transcendentals=0),
    )(block, wsum, *sofar)


def root_kernel(
    far_ref, wsum_ref, gram_ref, part_ref, out_ref, rhs_ref, bh, bl, t, p, ph, pl_, gh, gl, z, zh, zl
):
    obs_tile = far_ref.shape[1]
    patches, members = out_ref.shape[:2]
    inv = 1.0 / (members - 1)
    eye = (
        lax.broadcasted_iota(jnp.int32, (HALF, HALF), 0)
        == lax.broadcasted_iota(jnp.int32, (HALF, HALF), 1)
    ).astype(F32)

    def put(value, full, high, low, n, rows, cols):
        if full is not None:
            full[n, rows, cols] = value
        high[n, rows, cols], low[n, rows, cols] = split(value)

    def gram(n):
        spot = slice(2 * obs_tile, 3 * obs_tile)
        add_part(n, spot, far_ref, wsum_ref, bh, bl, gram_ref, part_ref, t, rhs_ref)
        rhs_ref[n] = rhs_ref[n] * inv

    def start(n):
        g00 = (t[n, LO, LO] + t[n, LO, LO].T) * inv + eye
        g01 = (t[n, LO, HI] + t[n, HI, LO].T) * inv
        g11 = (t[n, HI, HI] + t[n, HI, HI].T) * inv + eye
        g10 = g01.T
        rows0 = jnp.sum(jnp.abs(g00), 0, keepdims=True) + jnp.sum(jnp.abs(g10), 0, keepdims=True)
        rows1 = jnp.sum(jnp.abs(g01), 0, keepdims=True) + jnp.sum(jnp.abs(g11), 0, keepdims=True)
        scale = jnp.max(jnp.maximum(rows0, rows1), axis=1, keepdims=True)
        shrink = 1.0 / scale
        for rows, cols, g in ((LO, LO, g00), (LO, HI, g01), (HI, LO, g10), (HI, HI, g11)):
            cur = g * shrink
            put(cur, p, ph, pl_, n, rows, cols)
            first = -0.5 * cur
            if rows == cols:
                first = first + 1.5 * eye
            put(first, z, zh, zl, n, rows, cols)
        return scale

    def square(n):
        t[n, LO, LO] = 0.5 * mm(ph[n, LO, :], ph[n, :, LO]) + mm(ph[n, LO, :], pl_[n, :, LO])
        t[n, HI, LO] = mm(ph[n, HI, :], ph[n, :, LO]) + mm(ph[n, HI, :], pl_[n, :, LO])
        t[n, LO, HI] = mm(ph[n, LO, :], pl_[n, :, HI])
        t[n, HI, HI] = 0.5 * mm(ph[n, HI, :], ph[n, :, HI]) + mm(ph[n, HI, :], pl_[n, :, HI])

    def squared(n, one_pass):
        g00 = t[n, LO, LO] + t[n, LO, LO].T
        g10 = t[n, HI, LO] + t[n, LO, HI].T
        g11 = t[n, HI, HI] + t[n, HI, HI].T
        for rows, cols, g in ((LO, LO, g00), (HI, LO, g10), (LO, HI, g10.T), (HI, HI, g11)):
            if one_pass:
                gh[n, rows, cols] = g.astype(BF)
            else:
                put(g, None, gh, gl, n, rows, cols)
        p[n, LO, LO] = 2.25 * p[n, LO, LO] - 1.5 * g00
        p[n, HI, LO] = 2.25 * p[n, HI, LO] - 1.5 * g10
        p[n, HI, HI] = 2.25 * p[n, HI, HI] - 1.5 * g11

    def product(n, high, low, rows, cols):
        return (
            mm(ph[n, rows, :], high[n, :, cols])
            + mm(pl_[n, rows, :], high[n, :, cols])
            + mm(ph[n, rows, :], low[n, :, cols])
        )

    def factor(n):
        z00 = 1.5 * z[n, LO, LO] - 0.5 * product(n, zh, zl, LO, LO)
        z10 = 1.5 * z[n, HI, LO] - 0.5 * product(n, zh, zl, HI, LO)
        z11 = 1.5 * z[n, HI, HI] - 0.5 * product(n, zh, zl, HI, HI)
        return z00, z10, z11

    def few_factor(n, lead):
        gl[n, LO, LO] = (z[n, LO, LO] - lead * eye).astype(BF)
        gl[n, HI, LO] = z[n, HI, LO].astype(BF)
        gl[n, LO, HI] = z[n, HI, LO].T.astype(BF)
        gl[n, HI, HI] = (z[n, HI, HI] - lead * eye).astype(BF)

        def moved(rows, cols):
            part = lead * p[n, rows, cols] + mm(ph[n, rows, :], gl[n, :, cols])
            return 1.5 * z[n, rows, cols] - 0.5 * part

        return moved(LO, LO), moved(HI, LO), moved(HI, HI)

    def keep(n, parts):
        z00, z10, z11 = parts
        put(z00, z, zh, zl, n, LO, LO)
        put(z10, z, zh, zl, n, HI, LO)
        put(z10.T, None, zh, zl, n, LO, HI)
        put(z11, z, zh, zl, n, HI, HI)

    def cube(n, one_pass):
        def times(rows, cols):
            if one_pass:
                return mm(ph[n, rows, :], gh[n, :, cols])
            return product(n, gh, gl, rows, cols)

        n00 = p[n, LO, LO] + 0.25 * times(LO, LO)
        n10 = p[n, HI, LO] + 0.25 * times(HI, LO)
        n11 = p[n, HI, HI] + 0.25 * times(HI, HI)
        put(n00, p, ph, pl_, n, LO, LO)
        put(n10, p, ph, pl_, n, HI, LO)
        put(n10.T, None, ph, pl_, n, LO, HI)
        put(n11, p, ph, pl_, n, HI, HI)

    def mean_square(n):
        p00, p10, p11 = p[n, LO, LO], p[n, HI, LO], p[n, HI, HI]
        return jnp.sum(p00 * p00 + 2.0 * (p10 * p10) + p11 * p11) * (1.0 / members)

    def near_one(n):
        e10 = -p[n, HI, LO]
        gh[n, LO, LO] = (eye - p[n, LO, LO]).astype(BF)
        gh[n, HI, LO] = e10.astype(BF)
        gh[n, LO, HI] = e10.T.astype(BF)
        gh[n, HI, HI] = (eye - p[n, HI, HI]).astype(BF)

    def near_factor(n):
        z00 = z[n, LO, LO] + 0.5 * mm(gh[n, LO, :], zh[n, :, LO])
        z10 = z[n, HI, LO] + 0.5 * mm(gh[n, HI, :], zh[n, :, LO])
        z11 = z[n, HI, HI] + 0.5 * mm(gh[n, HI, :], zh[n, :, HI])
        return z00, z10, z11

    def near_square(n):
        t[n, LO, LO] = mm(gh[n, LO, :], gh[n, :, LO])
        t[n, HI, LO] = mm(gh[n, HI, :], gh[n, :, LO])
        t[n, HI, HI] = mm(gh[n, HI, :], gh[n, :, HI])

    def near_squared(n):
        gl[n, LO, LO] = t[n, LO, LO].astype(BF)
        gl[n, HI, LO] = t[n, HI, LO].astype(BF)
        gl[n, LO, HI] = t[n, HI, LO].T.astype(BF)
        gl[n, HI, HI] = t[n, HI, HI].astype(BF)

    def near_cube(n):
        e00 = 0.75 * t[n, LO, LO] + 0.25 * mm(gh[n, LO, :], gl[n, :, LO])
        e10 = 0.75 * t[n, HI, LO] + 0.25 * mm(gh[n, HI, :], gl[n, :, LO])
        e11 = 0.75 * t[n, HI, HI] + 0.25 * mm(gh[n, HI, :], gl[n, :, HI])
        put(eye - e00, p, ph, pl_, n, LO, LO)
        put(-e10, p, ph, pl_, n, HI, LO)
        put(-e10.T, None, ph, pl_, n, LO, HI)
        put(eye - e11, p, ph, pl_, n, HI, HI)

    every = range(patches)
    for n in every:
        gram(n)
    scales = [start(n) for n in every]

    def sweep(lead, one_pass):
        for n in every:
            square(n)
        for n in every:
            if one_pass and lead is not None:
                keep(n, few_factor(n, lead))
            squared(n, one_pass)
            if not one_pass and lead is not None:
                keep(n, factor(n))
            cube(n, one_pass)

    def near_sweep(one_pass):
        for n in every:
            near_one(n)
        for n in every:
            near_square(n)
        for n in every:
            near_squared(n)
            keep(n, near_factor(n) if one_pass else factor(n))
            near_cube(n)

    least = jnp.min(1.0 / jnp.concatenate(scales, 0))
    mean = mean_square(0)
    for n in range(1, patches):
        mean = jnp.maximum(mean, mean_square(n))
    count = sum((mean <= bound).astype(jnp.int32) for bound in SMALL)
    count = jnp.where(least >= 1.0 / NARROW, count, 0)

    def onward(value):
        return 0.25 * value * (3.0 - value) * (3.0 - value)

    @pl.when(count == 0)
    def _():
        sweep(None, False)

    @pl.when(count > 0)
    def _():
        sweep(None, True)

    def step(k, carry):
        least, lead = carry
        few = k < count
        rest = jnp.logical_not(few)
        wide = 1.0 - least

        @pl.when(few)
        def _():
            sweep(lead, True)

        @pl.when(jnp.logical_and(rest, wide > MID))
        def _():
            sweep(lead, False)

        @pl.when(jnp.logical_and(rest, jnp.logical_and(wide <= MID, wide > LOW)))
        def _():
            near_sweep(False)

        @pl.when(jnp.logical_and(rest, wide <= LOW))
        def _():
            near_sweep(True)

        return onward(least), 1.5 * lead

    least, _ = lax.fori_loop(1, NS_ITERS - 1, step, (onward(least), jnp.float32(1.5)))

    def finish(make):
        for n in every:
            z00, z10, z11 = make(n)
            out_ref[n, LO, LO] = z00 * lax.rsqrt(scales[n])
            out_ref[n, HI, LO] = z10 * lax.rsqrt(scales[n])
            out_ref[n, LO, HI] = z10.T * lax.rsqrt(scales[n])
            out_ref[n, HI, HI] = z11 * lax.rsqrt(scales[n])

    @pl.when(1.0 - least > LOW)
    def _():
        finish(factor)

    @pl.when(1.0 - least <= LOW)
    def _():
        for n in every:
            near_one(n)
        finish(near_factor)


def inverse_roots(near, own, far, wsum, members):
    sofar = gram_part(1, own, wsum, members)
    sofar = gram_part(0, near, wsum, members, sofar)
    patches, obs_tile = wsum.shape[0], far.shape[1]
    square = (patches, members, members)
    return pl.pallas_call(
        root_kernel,
        out_shape=(
            jax.ShapeDtypeStruct(square, F32),
            jax.ShapeDtypeStruct((patches, 8, members), F32),
        ),
        scratch_shapes=[
            pltpu.VMEM((patches, 2 * PAD + members, obs_tile), BF),
            pltpu.VMEM((patches, members, obs_tile), BF),
            pltpu.VMEM(square, F32),
            pltpu.VMEM(square, F32),
            pltpu.VMEM(square, BF),
            pltpu.VMEM(square, BF),
            pltpu.VMEM(square, BF),
            pltpu.VMEM(square, BF),
            pltpu.VMEM(square, F32),
            pltpu.VMEM(square, BF),
            pltpu.VMEM(square, BF),
        ],
        compiler_params=pltpu.CompilerParams(vmem_limit_bytes=28 * 1024 * 1024),
        cost_estimate=pl.CostEstimate(flops=25 * 10**9, bytes_accessed=4 * 10**6, transcendentals=0),
    )(far, wsum, *sofar)


def apply_kernel(root_ref, rhs_ref, cols_ref, out_ref):
    devices, patches, levels, mem_dev, nlat = cols_ref.shape
    members = devices * mem_dev
    for n in range(patches):
        root = root_ref[n]
        high, low = split(root)
        weight = jnp.sum(root * rhs_ref[n, 0:1, :], axis=1, keepdims=True)
        cols = jnp.concatenate(
            [cols_ref[:, n, lev].reshape(members, nlat) for lev in range(levels)], 1
        )
        center = jnp.sum(cols, axis=0, keepdims=True) * (1.0 / members)
        cols_high, cols_low = split(cols - center)
        moved = mm(high, cols_high) + mm(low, cols_high) + mm(high, cols_low)
        result = moved + (center + jnp.sum(moved * weight, axis=0, keepdims=True))
        for lev in range(levels):
            part = result[:, lev * nlat : (lev + 1) * nlat]
            out_ref[:, n, lev] = part.reshape(devices, mem_dev, nlat)


def apply_roots(roots, rhs, cols):
    return pl.pallas_call(
        apply_kernel,
        out_shape=jax.ShapeDtypeStruct(cols.shape, F32),
        compiler_params=pltpu.CompilerParams(vmem_limit_bytes=24 * 1024 * 1024),
        cost_estimate=pl.CostEstimate(flops=8 * 10**8, bytes_accessed=4 * 10**6, transcendentals=0),
    )(roots, rhs, cols)


def advance(field, west, courant):
    nlat = field.shape[1]
    lat = lax.broadcasted_iota(jnp.int32, field.shape, 1)
    upper = jnp.where(lat == nlat - 1, field, pltpu.roll(field, nlat - 1, 1))
    lower = jnp.where(lat == 0, field, pltpu.roll(field, 1, 1))
    return field - courant * (field - west) + DIFFUSE * (upper + lower - 2.0 * field)


def picker(cells, nlat):
    spot = (lax.broadcasted_iota(jnp.int32, (nlat, cells.shape[1]), 0) == cells % nlat).astype(BF)
    twice = jnp.concatenate([spot, spot], 0)
    return lambda value: mm(jnp.concatenate(split(value), 1), twice)


def inner_kernel(
    field_hbm, courant_hbm, cell_hbm, value_hbm, rinv_hbm, out_ref, edge_ref, message_ref, extra_ref,
    field_ref, courant_ref, cell_ref, value_ref, rinv_ref, sems
):
    copies = [
        pltpu.make_async_copy(source, target, sems.at[i])
        for i, (source, target) in enumerate(
            (
                (field_hbm, field_ref),
                (courant_hbm, courant_ref),
                (cell_hbm, cell_ref),
                (value_hbm, value_ref),
                (rinv_hbm, rinv_ref),
            )
        )
    ]
    for copy in copies:
        copy.start()
    for copy in copies:
        copy.wait()
    lines, levels, members, nlat = out_ref.shape
    cells = cell_ref[...]
    pick = picker(cells, nlat)
    source_row = cells // nlat
    obs = jnp.zeros((members, cells.shape[1]), F32)
    for lev in range(levels):
        courant = courant_ref[lev : lev + 1, :]
        old, old_next = None, None
        for line in range(lines):
            now = field_ref[pl.ds(lev * lines + line, members, stride=levels * lines), :]
            if line < NSTEP:
                edge_ref[line, lev] = now
            now_next = None
            if line >= 1:
                now_next = advance(now, old, courant)
            if line >= NSTEP:
                done = advance(now_next, old_next, courant)
                out_ref[line, lev] = done
                obs = jnp.where(source_row == lev * lines + line, pick(done), obs)
            old, old_next = now, now_next
    message_ref[0:members, :] = obs
    message_ref[members : members + 1, :] = value_ref[...]
    message_ref[members + 1 : members + 2, :] = rinv_ref[...]
    message_ref[members + 2 :, :] = jnp.zeros((6, obs.shape[1]), F32)
    extra_ref[...] = jnp.zeros(extra_ref.shape, jnp.int32)
    extra_ref[0:1, :] = cells
    edge_ref[NSTEP] = jnp.zeros(edge_ref.shape[1:], F32)
    for lev in range(levels):
        edge_ref[NSTEP, lev, 0:1, :] = courant_ref[lev : lev + 1, :]


def inner_forecast(members, courant, cells, value, rinv):
    mem_dev, levels, lines, nlat = members.shape
    rows = mem_dev * levels * lines
    nobs = cells.shape[1]
    return pl.pallas_call(
        inner_kernel,
        out_shape=(
            jax.ShapeDtypeStruct((lines, levels, mem_dev, nlat), F32),
            jax.ShapeDtypeStruct((NSTEP + 1, levels, mem_dev, nlat), F32),
            jax.ShapeDtypeStruct((mem_dev + 8, nobs), F32),
            jax.ShapeDtypeStruct((8, nobs), jnp.int32),
        ),
        in_specs=[pl.BlockSpec(memory_space=pltpu.HBM)] * 5,
        scratch_shapes=[
            pltpu.VMEM((rows, nlat), F32),
            pltpu.VMEM(courant.shape, F32),
            pltpu.VMEM(cells.shape, jnp.int32),
            pltpu.VMEM(value.shape, F32),
            pltpu.VMEM(rinv.shape, F32),
            pltpu.SemaphoreType.DMA((5,)),
        ],
        compiler_params=pltpu.CompilerParams(vmem_limit_bytes=60 * 1024 * 1024),
        cost_estimate=pl.CostEstimate(flops=10**8, bytes_accessed=2 * 10**6, transcendentals=0),
    )(members.reshape(rows, nlat), courant, cells, value, rinv)


def edge_kernel(lines, halo_ref, edge_ref, cell_ref, partial_ref, field_ref, out_ref, message_ref):
    del field_ref
    _, levels, members, nlat = edge_ref.shape
    cells = cell_ref[0:1, :]
    pick = picker(cells, nlat)
    source_row = cells // nlat
    obs = partial_ref[0:members, :]
    for lev in range(levels):
        courant = edge_ref[NSTEP, lev, 0:1, :]
        old = halo_ref[1, lev]
        old_next = advance(old, halo_ref[0, lev], courant)
        for line in range(NSTEP):
            now = edge_ref[line, lev]
            now_next = advance(now, old, courant)
            done = advance(now_next, old_next, courant)
            out_ref[line, lev] = done
            obs = jnp.where(source_row == lev * lines + line, pick(done), obs)
            old, old_next = now, now_next
    value, rinv = partial_ref[members : members + 1, :], partial_ref[members + 1 : members + 2, :]
    message_ref[...] = jnp.sqrt(rinv) * (obs - value)


def edge_forecast(halo, edge, cells, partial, field):
    lines, levels, mem_dev, nlat = field.shape

    def whole(array):
        zeros = (0,) * array.ndim
        return pl.BlockSpec(array.shape, lambda i: zeros)

    first = pl.BlockSpec((NSTEP, levels, mem_dev, nlat), lambda i: (0, 0, 0, 0))
    small = (halo, edge, cells, partial)
    message = (mem_dev, partial.shape[1])
    return pl.pallas_call(
        functools.partial(edge_kernel, lines),
        grid=(1,),
        out_shape=(
            jax.ShapeDtypeStruct(field.shape, F32),
            jax.ShapeDtypeStruct(message, F32),
        ),
        in_specs=[whole(a) for a in small] + [pl.BlockSpec(memory_space=pl.ANY)],
        out_specs=(first, pl.BlockSpec(message, lambda i: (0, 0))),
        input_output_aliases={len(small): 0},
        compiler_params=pltpu.CompilerParams(vmem_limit_bytes=60 * 1024 * 1024),
        cost_estimate=pl.CostEstimate(flops=10**7, bytes_accessed=10**6, transcendentals=0),
    )(*small, field)


def restore_kernel(part_ref, out_hbm, out_ref, sems):
    devices, patches, levels, mem_dev, nlat = part_ref.shape
    lines = patches * devices
    group = 8
    copies = []
    for i in range(mem_dev // group):
        for device in range(devices):
            for n in range(patches):
                for lev in range(levels):
                    first = i * group * levels * lines + lev * lines + patches * device + n
                    rows = pl.ds(first, group, stride=levels * lines)
                    out_ref[rows, :] = part_ref[device, n, lev, i * group : (i + 1) * group, :]
        spot = pl.ds(i * group * levels * lines, group * levels * lines)
        copies.append(pltpu.make_async_copy(out_ref.at[spot], out_hbm.at[spot], sems.at[i]))
        copies[-1].start()
    for copy in copies:
        copy.wait()


def restore(parts):
    devices, patches, levels, mem_dev, nlat = parts.shape
    rows = mem_dev * levels * patches * devices
    out = pl.pallas_call(
        restore_kernel,
        out_shape=jax.ShapeDtypeStruct((rows, nlat), F32),
        in_specs=[pl.BlockSpec(memory_space=pltpu.VMEM)],
        out_specs=pl.BlockSpec(memory_space=pl.ANY),
        scratch_shapes=[
            pltpu.VMEM((rows, nlat), F32),
            pltpu.SemaphoreType.DMA((mem_dev // 8,)),
        ],
        compiler_params=pltpu.CompilerParams(vmem_limit_bytes=24 * 1024 * 1024),
    )(parts)
    return out.reshape(mem_dev, levels, patches * devices, nlat)


def shifted(value, axis, steps):
    count = lax.axis_size(axis)
    pairs = [(source, (source + steps) % count) for source in range(count)]
    return lax.ppermute(value, axis, pairs)


def neighbours(value):
    mem, tile = lax.axis_size("mem"), lax.axis_size("tile")
    pairs = [
        (m * tile + t, m * tile + (t + (1 if m % 2 == 0 else -1)) % tile)
        for m in range(mem)
        for t in range(tile)
    ]
    near = lax.ppermute(value, ("mem", "tile"), pairs)
    far = lax.ppermute(near, "mem", [(m, m ^ 1) for m in range(mem)])
    return near, far


def on_device(
    members, courant, obs_cell, obs_value, obs_rinv, nbr_obs, nbr_class, nbr_count, loc_table
):
    mem_dev, levels, lines, nlat = members.shape
    devices = lax.axis_size("mem")
    obs_tile = obs_cell.shape[0]
    slots = nbr_obs.shape[1]
    edge = jnp.transpose(members[:, :, lines - NSTEP :, :], (2, 1, 0, 3))
    halo = shifted(edge, "tile", 1)
    field, first_lines, partial, cells = inner_forecast(
        members, courant, obs_cell[None], obs_value[None], obs_rinv[None]
    )
    field, message = edge_forecast(halo, first_lines, cells, partial, field)
    own = lax.all_gather(message, "mem", axis=0, tiled=True)
    own, nbr_obs, nbr_class, nbr_count, loc_table, field = lax.optimization_barrier(
        (own, nbr_obs, nbr_class, nbr_count, loc_table, field)
    )
    near, far = neighbours(own)
    columns = lax.all_to_all(
        field.reshape(devices, lines // devices, levels, mem_dev, nlat), "mem", 0, 0, tiled=True
    )
    tile_index = lax.axis_index("tile")
    tile_count = lax.axis_size("tile")
    offset = (nbr_obs // obs_tile - tile_index + 1) % tile_count
    offset = jnp.where(lax.axis_index("mem") % 2 == 0, offset, 2 - offset)
    local_ids = offset * obs_tile + nbr_obs % obs_tile
    classes = jnp.arange(loc_table.shape[0])
    local_w = jnp.sum(jnp.where(nbr_class[..., None] == classes, loc_table, 0.0), -1)
    local_w = jnp.where(jnp.arange(slots) < nbr_count[:, None], local_w, 0.0)
    places = jnp.arange(3 * obs_tile)
    wsum = jnp.sum(jnp.where(local_ids[:, :, None] == places, local_w[:, :, None], 0.0), 1)

    roots, rhs = inverse_roots(near, own, far, wsum, devices * mem_dev)
    parts = apply_roots(roots, rhs, columns)
    return restore(lax.all_to_all(parts, "mem", 0, 0, tiled=True))


def solution(mesh):
    return jax.shard_map(
        on_device,
        mesh=mesh,
        in_specs=(
            P("mem", None, "tile", None),
            P(),
            P("tile"),
            P("tile"),
            P("tile"),
            P(("tile", "mem"), None),
            P(("tile", "mem"), None),
            P(("tile", "mem")),
            P(),
        ),
        out_specs=P("mem", None, "tile", None),
        check_vma=False,
    )
```

```python
import functools
import jax
import jax.numpy as jnp
from jax import lax
from jax.experimental import pallas as pl
from jax.experimental.pallas import tpu as pltpu
from jax.sharding import PartitionSpec as P

NSTEP = 2
NS_ITERS = 8
DIFFUSE = 0.1
HALF = 256
PAD = 16
NARROW = 32.0
SMALL = (1.0 / 5, 1.0 / 16, 1.0 / 64)
MID, LOW = 1.0 / 4, 1.0 / 32
BF = jnp.bfloat16
F32 = jnp.float32
LO, HI = slice(0, HALF), slice(HALF, 2 * HALF)


def split(value):
    high = value.astype(BF)
    return high, (value - high.astype(F32)).astype(BF)


def mm(left, right):
    return jnp.dot(left, right, preferred_element_type=F32)


def mm_t(left, right):
    return lax.dot_general(left, right, (((1,), (1,)), ((), ())), preferred_element_type=F32)


def add_part(n, spot, block_ref, wsum_ref, bh, bl, old, old_rhs, new, new_rhs):
    members, obs_tile = block_ref.shape
    top = 2 * PAD
    block = block_ref[...]
    mean = jnp.sum(block, axis=0, keepdims=True) * (1.0 / members)
    total = wsum_ref[n : n + 1, spot]
    root = jnp.where(total > 0.0, jnp.sqrt(jnp.maximum(total, 1e-30)), 0.0)
    row = jnp.broadcast_to(-root * mean, (PAD, obs_tile))
    bh[n, 0:PAD, :], bh[n, PAD:top, :] = split(row)
    bh[n, top:, :], bl[n] = split((block - mean) * root)
    first = bh[n, 0 : top + HALF, :]
    second = bh[n, top + HALF :, :]
    left = mm_t(first, first[top:, :])
    right = mm_t(first, second)
    left_low = mm_t(first, bl[n, LO, :])
    right_low = mm_t(first, bl[n, HI, :])
    sums = {
        (0, 0): 0.5 * left[top:] + left_low[top:],
        (0, 1): right[top:] + right_low[top:],
        (1, 0): mm_t(second, bl[n, LO, :]),
        (1, 1): 0.5 * mm_t(second, second) + mm_t(second, bl[n, HI, :]),
    }
    for (a, b), value in sums.items():
        spot_a, spot_b = (LO, HI)[a], (LO, HI)[b]
        new[n, spot_a, spot_b] = value if old is None else value + old[n, spot_a, spot_b]
    for spot_b, high, low in ((LO, left, left_low), (HI, right, right_low)):
        rhs = jnp.broadcast_to(high[0:1] + high[PAD : PAD + 1] + low[0:1], (8, HALF))
        new_rhs[n, :, spot_b] = rhs if old_rhs is None else rhs + old_rhs[n, :, spot_b]


def part_kernel(spot, block_ref, wsum_ref, *refs):
    old, old_rhs = refs[:-4] if len(refs) == 6 else (None, None)
    new, new_rhs, bh, bl = refs[-4:]
    for n in range(new.shape[0]):
        add_part(n, spot, block_ref, wsum_ref, bh, bl, old, old_rhs, new, new_rhs)


def gram_part(which, block, wsum, members, sofar=()):
    patches, obs_tile = wsum.shape[0], block.shape[1]
    spot = slice(which * obs_tile, (which + 1) * obs_tile)
    return pl.pallas_call(
        functools.partial(part_kernel, spot),
        out_shape=(
            jax.ShapeDtypeStruct((patches, members, members), F32),
            jax.ShapeDtypeStruct((patches, 8, members), F32),
        ),
        scratch_shapes=[
            pltpu.VMEM((patches, 2 * PAD + members, obs_tile), BF),
            pltpu.VMEM((patches, members, obs_tile), BF),
        ],
        compiler_params=pltpu.CompilerParams(vmem_limit_bytes=24 * 1024 * 1024),
        cost_estimate=pl.CostEstimate(flops=2 * 10**9, bytes_accessed=4 * 10**6, transcendentals=0),
    )(block, wsum, *sofar)


def root_kernel(
    far_ref, wsum_ref, gram_ref, part_ref, out_ref, rhs_ref, bh, bl, t, p, ph, pl_, gh, gl, z, zh, zl
):
    obs_tile = far_ref.shape[1]
    patches, members = out_ref.shape[:2]
    inv = 1.0 / (members - 1)
    eye = (
        lax.broadcasted_iota(jnp.int32, (HALF, HALF), 0)
        == lax.broadcasted_iota(jnp.int32, (HALF, HALF), 1)
    ).astype(F32)

    def put(value, full, high, low, n, rows, cols):
        if full is not None:
            full[n, rows, cols] = value
        high[n, rows, cols], low[n, rows, cols] = split(value)

    def gram(n):
        spot = slice(2 * obs_tile, 3 * obs_tile)
        add_part(n, spot, far_ref, wsum_ref, bh, bl, gram_ref, part_ref, t, rhs_ref)
        rhs_ref[n] = rhs_ref[n] * inv

    def start(n):
        g00 = (t[n, LO, LO] + t[n, LO, LO].T) * inv + eye
        g01 = (t[n, LO, HI] + t[n, HI, LO].T) * inv
        g11 = (t[n, HI, HI] + t[n, HI, HI].T) * inv + eye
        g10 = g01.T
        rows0 = jnp.sum(jnp.abs(g00), 0, keepdims=True) + jnp.sum(jnp.abs(g10), 0, keepdims=True)
        rows1 = jnp.sum(jnp.abs(g01), 0, keepdims=True) + jnp.sum(jnp.abs(g11), 0, keepdims=True)
        scale = jnp.max(jnp.maximum(rows0, rows1), axis=1, keepdims=True)
        shrink = 1.0 / scale
        for rows, cols, g in ((LO, LO, g00), (LO, HI, g01), (HI, LO, g10), (HI, HI, g11)):
            cur = g * shrink
            put(cur, p, ph, pl_, n, rows, cols)
            first = -0.5 * cur
            if rows == cols:
                first = first + 1.5 * eye
            put(first, z, zh, zl, n, rows, cols)
        return scale

    def square(n):
        t[n, LO, LO] = 0.5 * mm(ph[n, LO, :], ph[n, :, LO]) + mm(ph[n, LO, :], pl_[n, :, LO])
        t[n, HI, LO] = mm(ph[n, HI, :], ph[n, :, LO]) + mm(ph[n, HI, :], pl_[n, :, LO])
        t[n, LO, HI] = mm(ph[n, LO, :], pl_[n, :, HI])
        t[n, HI, HI] = 0.5 * mm(ph[n, HI, :], ph[n, :, HI]) + mm(ph[n, HI, :], pl_[n, :, HI])

    def squared(n, one_pass):
        g00 = t[n, LO, LO] + t[n, LO, LO].T
        g10 = t[n, HI, LO] + t[n, LO, HI].T
        g11 = t[n, HI, HI] + t[n, HI, HI].T
        for rows, cols, g in ((LO, LO, g00), (HI, LO, g10), (LO, HI, g10.T), (HI, HI, g11)):
            if one_pass:
                gh[n, rows, cols] = g.astype(BF)
            else:
                put(g, None, gh, gl, n, rows, cols)
        p[n, LO, LO] = 2.25 * p[n, LO, LO] - 1.5 * g00
        p[n, HI, LO] = 2.25 * p[n, HI, LO] - 1.5 * g10
        p[n, HI, HI] = 2.25 * p[n, HI, HI] - 1.5 * g11

    def product(n, high, low, rows, cols):
        return (
            mm(ph[n, rows, :], high[n, :, cols])
            + mm(pl_[n, rows, :], high[n, :, cols])
            + mm(ph[n, rows, :], low[n, :, cols])
        )

    def factor(n):
        z00 = 1.5 * z[n, LO, LO] - 0.5 * product(n, zh, zl, LO, LO)
        z10 = 1.5 * z[n, HI, LO] - 0.5 * product(n, zh, zl, HI, LO)
        z11 = 1.5 * z[n, HI, HI] - 0.5 * product(n, zh, zl, HI, HI)
        return z00, z10, z11

    def few_factor(n, lead):
        gl[n, LO, LO] = (z[n, LO, LO] - lead * eye).astype(BF)
        gl[n, HI, LO] = z[n, HI, LO].astype(BF)
        gl[n, LO, HI] = z[n, HI, LO].T.astype(BF)
        gl[n, HI, HI] = (z[n, HI, HI] - lead * eye).astype(BF)

        def moved(rows, cols):
            part = lead * p[n, rows, cols] + mm(ph[n, rows, :], gl[n, :, cols])
            return 1.5 * z[n, rows, cols] - 0.5 * part

        return moved(LO, LO), moved(HI, LO), moved(HI, HI)

    def keep(n, parts):
        z00, z10, z11 = parts
        put(z00, z, zh, zl, n, LO, LO)
        put(z10, z, zh, zl, n, HI, LO)
        put(z10.T, None, zh, zl, n, LO, HI)
        put(z11, z, zh, zl, n, HI, HI)

    def cube(n, one_pass):
        def times(rows, cols):
            if one_pass:
                return mm(ph[n, rows, :], gh[n, :, cols])
            return product(n, gh, gl, rows, cols)

        n00 = p[n, LO, LO] + 0.25 * times(LO, LO)
        n10 = p[n, HI, LO] + 0.25 * times(HI, LO)
        n11 = p[n, HI, HI] + 0.25 * times(HI, HI)
        put(n00, p, ph, pl_, n, LO, LO)
        put(n10, p, ph, pl_, n, HI, LO)
        put(n10.T, None, ph, pl_, n, LO, HI)
        put(n11, p, ph, pl_, n, HI, HI)

    def mean_square(n):
        p00, p10, p11 = p[n, LO, LO], p[n, HI, LO], p[n, HI, HI]
        return jnp.sum(p00 * p00 + 2.0 * (p10 * p10) + p11 * p11) * (1.0 / members)

    def near_one(n):
        e10 = -p[n, HI, LO]
        gh[n, LO, LO] = (eye - p[n, LO, LO]).astype(BF)
        gh[n, HI, LO] = e10.astype(BF)
        gh[n, LO, HI] = e10.T.astype(BF)
        gh[n, HI, HI] = (eye - p[n, HI, HI]).astype(BF)

    def near_factor(n):
        z00 = z[n, LO, LO] + 0.5 * mm(gh[n, LO, :], zh[n, :, LO])
        z10 = z[n, HI, LO] + 0.5 * mm(gh[n, HI, :], zh[n, :, LO])
        z11 = z[n, HI, HI] + 0.5 * mm(gh[n, HI, :], zh[n, :, HI])
        return z00, z10, z11

    def near_square(n):
        t[n, LO, LO] = mm(gh[n, LO, :], gh[n, :, LO])
        t[n, HI, LO] = mm(gh[n, HI, :], gh[n, :, LO])
        t[n, HI, HI] = mm(gh[n, HI, :], gh[n, :, HI])

    def near_squared(n):
        gl[n, LO, LO] = t[n, LO, LO].astype(BF)
        gl[n, HI, LO] = t[n, HI, LO].astype(BF)
        gl[n, LO, HI] = t[n, HI, LO].T.astype(BF)
        gl[n, HI, HI] = t[n, HI, HI].astype(BF)

    def near_cube(n):
        e00 = 0.75 * t[n, LO, LO] + 0.25 * mm(gh[n, LO, :], gl[n, :, LO])
        e10 = 0.75 * t[n, HI, LO] + 0.25 * mm(gh[n, HI, :], gl[n, :, LO])
        e11 = 0.75 * t[n, HI, HI] + 0.25 * mm(gh[n, HI, :], gl[n, :, HI])
        put(eye - e00, p, ph, pl_, n, LO, LO)
        put(-e10, p, ph, pl_, n, HI, LO)
        put(-e10.T, None, ph, pl_, n, LO, HI)
        put(eye - e11, p, ph, pl_, n, HI, HI)

    every = range(patches)
    for n in every:
        gram(n)
    scales = [start(n) for n in every]

    def sweep(lead, one_pass):
        for n in every:
            square(n)
        for n in every:
            if one_pass and lead is not None:
                keep(n, few_factor(n, lead))
            squared(n, one_pass)
            if not one_pass and lead is not None:
                keep(n, factor(n))
            cube(n, one_pass)

    def near_sweep(one_pass):
        for n in every:
            near_one(n)
        for n in every:
            near_square(n)
        for n in every:
            near_squared(n)
            keep(n, near_factor(n) if one_pass else factor(n))
            near_cube(n)

    least = jnp.min(1.0 / jnp.concatenate(scales, 0))
    mean = mean_square(0)
    for n in range(1, patches):
        mean = jnp.maximum(mean, mean_square(n))
    count = sum((mean <= bound).astype(jnp.int32) for bound in SMALL)
    count = jnp.where(least >= 1.0 / NARROW, count, 0)

    def onward(value):
        return 0.25 * value * (3.0 - value) * (3.0 - value)

    @pl.when(count == 0)
    def _():
        sweep(None, False)

    @pl.when(count > 0)
    def _():
        sweep(None, True)

    def step(k, carry):
        least, lead = carry
        few = k < count
        rest = jnp.logical_not(few)
        wide = 1.0 - least

        @pl.when(few)
        def _():
            sweep(lead, True)

        @pl.when(jnp.logical_and(rest, wide > MID))
        def _():
            sweep(lead, False)

        @pl.when(jnp.logical_and(rest, jnp.logical_and(wide <= MID, wide > LOW)))
        def _():
            near_sweep(False)

        @pl.when(jnp.logical_and(rest, wide <= LOW))
        def _():
            near_sweep(True)

        return onward(least), 1.5 * lead

    least, _ = lax.fori_loop(1, NS_ITERS - 1, step, (onward(least), jnp.float32(1.5)))

    def finish(make):
        for n in every:
            z00, z10, z11 = make(n)
            out_ref[n, LO, LO] = z00 * lax.rsqrt(scales[n])
            out_ref[n, HI, LO] = z10 * lax.rsqrt(scales[n])
            out_ref[n, LO, HI] = z10.T * lax.rsqrt(scales[n])
            out_ref[n, HI, HI] = z11 * lax.rsqrt(scales[n])

    @pl.when(1.0 - least > LOW)
    def _():
        finish(factor)

    @pl.when(1.0 - least <= LOW)
    def _():
        for n in every:
            near_one(n)
        finish(near_factor)


def inverse_roots(near, own, far, wsum, members):
    sofar = gram_part(1, own, wsum, members)
    sofar = gram_part(0, near, wsum, members, sofar)
    patches, obs_tile = wsum.shape[0], far.shape[1]
    square = (patches, members, members)
    return pl.pallas_call(
        root_kernel,
        out_shape=(
            jax.ShapeDtypeStruct(square, F32),
            jax.ShapeDtypeStruct((patches, 8, members), F32),
        ),
        scratch_shapes=[
            pltpu.VMEM((patches, 2 * PAD + members, obs_tile), BF),
            pltpu.VMEM((patches, members, obs_tile), BF),
            pltpu.VMEM(square, F32),
            pltpu.VMEM(square, F32),
            pltpu.VMEM(square, BF),
            pltpu.VMEM(square, BF),
            pltpu.VMEM(square, BF),
            pltpu.VMEM(square, BF),
            pltpu.VMEM(square, F32),
            pltpu.VMEM(square, BF),
            pltpu.VMEM(square, BF),
        ],
        compiler_params=pltpu.CompilerParams(vmem_limit_bytes=28 * 1024 * 1024),
        cost_estimate=pl.CostEstimate(flops=25 * 10**9, bytes_accessed=4 * 10**6, transcendentals=0),
    )(far, wsum, *sofar)


def apply_kernel(root_ref, rhs_ref, cols_ref, out_ref):
    devices, patches, levels, mem_dev, nlat = cols_ref.shape
    members = devices * mem_dev
    for n in range(patches):
        root = root_ref[n]
        high, low = split(root)
        weight = jnp.sum(root * rhs_ref[n, 0:1, :], axis=1, keepdims=True)
        cols = jnp.concatenate(
            [cols_ref[:, n, lev].reshape(members, nlat) for lev in range(levels)], 1
        )
        center = jnp.sum(cols, axis=0, keepdims=True) * (1.0 / members)
        cols_high, cols_low = split(cols - center)
        moved = mm(high, cols_high) + mm(low, cols_high) + mm(high, cols_low)
        result = moved + (center + jnp.sum(moved * weight, axis=0, keepdims=True))
        for lev in range(levels):
            part = result[:, lev * nlat : (lev + 1) * nlat]
            out_ref[:, n, lev] = part.reshape(devices, mem_dev, nlat)


def apply_roots(roots, rhs, cols):
    return pl.pallas_call(
        apply_kernel,
        out_shape=jax.ShapeDtypeStruct(cols.shape, F32),
        compiler_params=pltpu.CompilerParams(vmem_limit_bytes=24 * 1024 * 1024),
        cost_estimate=pl.CostEstimate(flops=8 * 10**8, bytes_accessed=4 * 10**6, transcendentals=0),
    )(roots, rhs, cols)


def advance(field, west, courant):
    nlat = field.shape[1]
    lat = lax.broadcasted_iota(jnp.int32, field.shape, 1)
    upper = jnp.where(lat == nlat - 1, field, pltpu.roll(field, nlat - 1, 1))
    lower = jnp.where(lat == 0, field, pltpu.roll(field, 1, 1))
    return field - courant * (field - west) + DIFFUSE * (upper + lower - 2.0 * field)


def picker(cells, nlat):
    spot = (lax.broadcasted_iota(jnp.int32, (nlat, cells.shape[1]), 0) == cells % nlat).astype(BF)
    twice = jnp.concatenate([spot, spot], 0)
    return lambda value: mm(jnp.concatenate(split(value), 1), twice)


def inner_kernel(field_ref, pack_ref, out_ref, edge_ref, obs_ref):
    lines, levels, members, nlat = out_ref.shape
    cells = pack_ref[2:3, :].astype(jnp.int32)
    pick = picker(cells, nlat)
    source_row = cells // nlat
    obs = jnp.zeros(obs_ref.shape, F32)
    for lev in range(levels):
        courant = pack_ref[3:4, lev * nlat : (lev + 1) * nlat]
        old, old_next = None, None
        for line in range(lines):
            now = field_ref[pl.ds(lev * lines + line, members, stride=levels * lines), :]
            if line < NSTEP:
                edge_ref[line, lev] = now
            now_next = None
            if line >= 1:
                now_next = advance(now, old, courant)
            if line >= NSTEP:
                done = advance(now_next, old_next, courant)
                out_ref[line, lev] = done
                obs = jnp.where(source_row == lev * lines + line, pick(done), obs)
            old, old_next = now, now_next
    obs_ref[...] = obs


def inner_forecast(members, pack):
    mem_dev, levels, lines, nlat = members.shape
    rows = mem_dev * levels * lines
    return pl.pallas_call(
        inner_kernel,
        out_shape=(
            jax.ShapeDtypeStruct((lines, levels, mem_dev, nlat), F32),
            jax.ShapeDtypeStruct((NSTEP, levels, mem_dev, nlat), F32),
            jax.ShapeDtypeStruct((mem_dev, pack.shape[1]), F32),
        ),
        compiler_params=pltpu.CompilerParams(vmem_limit_bytes=24 * 1024 * 1024),
        cost_estimate=pl.CostEstimate(flops=10**8, bytes_accessed=2 * 10**6, transcendentals=0),
    )(members.reshape(rows, nlat), pack)


def edge_kernel(lines, halo_ref, edge_ref, pack_ref, partial_ref, field_ref, out_ref, message_ref):
    del field_ref
    _, levels, members, nlat = edge_ref.shape
    cells = pack_ref[2:3, :].astype(jnp.int32)
    pick = picker(cells, nlat)
    source_row = cells // nlat
    obs = partial_ref[...]
    for lev in range(levels):
        courant = pack_ref[3:4, lev * nlat : (lev + 1) * nlat]
        old = halo_ref[1, lev]
        old_next = advance(old, halo_ref[0, lev], courant)
        for line in range(NSTEP):
            now = edge_ref[line, lev]
            now_next = advance(now, old, courant)
            done = advance(now_next, old_next, courant)
            out_ref[line, lev] = done
            obs = jnp.where(source_row == lev * lines + line, pick(done), obs)
            old, old_next = now, now_next
    message_ref[...] = jnp.sqrt(pack_ref[1:2, :]) * (obs - pack_ref[0:1, :])


def edge_forecast(halo, edge, pack, partial, field):
    lines, levels, mem_dev, nlat = field.shape

    def whole(array):
        zeros = (0,) * array.ndim
        return pl.BlockSpec(array.shape, lambda i: zeros)

    first = pl.BlockSpec((NSTEP, levels, mem_dev, nlat), lambda i: (0, 0, 0, 0))
    small = (halo, edge, pack, partial)
    return pl.pallas_call(
        functools.partial(edge_kernel, lines),
        grid=(1,),
        out_shape=(
            jax.ShapeDtypeStruct(field.shape, F32),
            jax.ShapeDtypeStruct(partial.shape, F32),
        ),
        in_specs=[whole(a) for a in small] + [pl.BlockSpec(memory_space=pl.ANY)],
        out_specs=(first, whole(partial)),
        input_output_aliases={len(small): 0},
        compiler_params=pltpu.CompilerParams(vmem_limit_bytes=24 * 1024 * 1024),
        cost_estimate=pl.CostEstimate(flops=10**7, bytes_accessed=10**6, transcendentals=0),
    )(*small, field)


def restore_kernel(part_ref, out_hbm, out_ref, sems):
    devices, patches, levels, mem_dev, nlat = part_ref.shape
    lines = patches * devices
    group = 8
    copies = []
    for i in range(mem_dev // group):
        for device in range(devices):
            for n in range(patches):
                for lev in range(levels):
                    first = i * group * levels * lines + lev * lines + patches * device + n
                    rows = pl.ds(first, group, stride=levels * lines)
                    out_ref[rows, :] = part_ref[device, n, lev, i * group : (i + 1) * group, :]
        spot = pl.ds(i * group * levels * lines, group * levels * lines)
        copies.append(pltpu.make_async_copy(out_ref.at[spot], out_hbm.at[spot], sems.at[i]))
        copies[-1].start()
    for copy in copies:
        copy.wait()


def restore(parts):
    devices, patches, levels, mem_dev, nlat = parts.shape
    rows = mem_dev * levels * patches * devices
    out = pl.pallas_call(
        restore_kernel,
        out_shape=jax.ShapeDtypeStruct((rows, nlat), F32),
        in_specs=[pl.BlockSpec(memory_space=pltpu.VMEM)],
        out_specs=pl.BlockSpec(memory_space=pl.ANY),
        scratch_shapes=[
            pltpu.VMEM((rows, nlat), F32),
            pltpu.SemaphoreType.DMA((mem_dev // 8,)),
        ],
        compiler_params=pltpu.CompilerParams(vmem_limit_bytes=24 * 1024 * 1024),
    )(parts)
    return out.reshape(mem_dev, levels, patches * devices, nlat)


def shifted(value, axis, steps):
    count = lax.axis_size(axis)
    pairs = [(source, (source + steps) % count) for source in range(count)]
    return lax.ppermute(value, axis, pairs)


def neighbours(value):
    mem, tile = lax.axis_size("mem"), lax.axis_size("tile")
    pairs = [
        (m * tile + t, m * tile + (t + (1 if m % 2 == 0 else -1)) % tile)
        for m in range(mem)
        for t in range(tile)
    ]
    near = lax.ppermute(value, ("mem", "tile"), pairs)
    far = lax.ppermute(near, "mem", [(m, m ^ 1) for m in range(mem)])
    return near, far


def on_device(
    members, courant, obs_cell, obs_value, obs_rinv, nbr_obs, nbr_class, nbr_count, loc_table
):
    mem_dev, levels, lines, nlat = members.shape
    devices = lax.axis_size("mem")
    obs_tile = obs_cell.shape[0]
    slots = nbr_obs.shape[1]
    edge = jnp.transpose(members[:, :, lines - NSTEP :, :], (2, 1, 0, 3))
    halo = shifted(edge, "tile", 1)
    rows = [obs_value, obs_rinv, obs_cell.astype(F32), courant.reshape(-1)]
    pack = jnp.concatenate([row[None] for row in rows] + [jnp.zeros((4, obs_tile), F32)], 0)
    field, first_lines, partial = inner_forecast(members, pack)
    field, message = edge_forecast(halo, first_lines, pack, partial, field)
    own = lax.all_gather(message, "mem", axis=0, tiled=True)
    own, nbr_obs, nbr_class, nbr_count, loc_table, field = lax.optimization_barrier(
        (own, nbr_obs, nbr_class, nbr_count, loc_table, field)
    )
    near, far = neighbours(own)
    columns = lax.all_to_all(
        field.reshape(devices, lines // devices, levels, mem_dev, nlat), "mem", 0, 0, tiled=True
    )
    tile_index = lax.axis_index("tile")
    tile_count = lax.axis_size("tile")
    offset = (nbr_obs // obs_tile - tile_index + 1) % tile_count
    offset = jnp.where(lax.axis_index("mem") % 2 == 0, offset, 2 - offset)
    local_ids = offset * obs_tile + nbr_obs % obs_tile
    classes = jnp.arange(loc_table.shape[0])
    local_w = jnp.sum(jnp.where(nbr_class[..., None] == classes, loc_table, 0.0), -1)
    local_w = jnp.where(jnp.arange(slots) < nbr_count[:, None], local_w, 0.0)
    places = jnp.arange(3 * obs_tile)
    wsum = jnp.sum(jnp.where(local_ids[:, :, None] == places, local_w[:, :, None], 0.0), 1)

    roots, rhs = inverse_roots(near, own, far, wsum, devices * mem_dev)
    parts = apply_roots(roots, rhs, columns)
    return restore(lax.all_to_all(parts, "mem", 0, 0, tiled=True))


def solution(mesh):
    return jax.shard_map(
        on_device,
        mesh=mesh,
        in_specs=(
            P("mem", None, "tile", None),
            P(),
            P("tile"),
            P("tile"),
            P("tile"),
            P(("tile", "mem"), None),
            P(("tile", "mem"), None),
            P(("tile", "mem")),
            P(),
        ),
        out_specs=P("mem", None, "tile", None),
        check_vma=False,
    )
```

```python
import functools
import jax
import jax.numpy as jnp
from jax import lax
from jax.experimental import pallas as pl
from jax.experimental.pallas import tpu as pltpu
from jax.sharding import PartitionSpec as P

NSTEP = 2
NS_ITERS = 8
DIFFUSE = 0.1
HALF = 256
PAD = 16
NARROW = 32.0
SMALL = (1.0 / 5, 1.0 / 16, 1.0 / 64)
MID, LOW = 1.0 / 4, 1.0 / 32
BF = jnp.bfloat16
F32 = jnp.float32
LO, HI = slice(0, HALF), slice(HALF, 2 * HALF)


def split(value):
    high = value.astype(BF)
    return high, (value - high.astype(F32)).astype(BF)


def mm(left, right):
    return jnp.dot(left, right, preferred_element_type=F32)


def mm_t(left, right):
    return lax.dot_general(left, right, (((1,), (1,)), ((), ())), preferred_element_type=F32)


def add_part(n, spot, block_ref, wsum_ref, bh, bl, old, old_rhs, new, new_rhs):
    members, obs_tile = block_ref.shape
    top = 2 * PAD
    block = block_ref[...]
    mean = jnp.sum(block, axis=0, keepdims=True) * (1.0 / members)
    total = wsum_ref[n : n + 1, spot]
    root = jnp.where(total > 0.0, jnp.sqrt(jnp.maximum(total, 1e-30)), 0.0)
    row = jnp.broadcast_to(-root * mean, (PAD, obs_tile))
    bh[n, 0:PAD, :], bh[n, PAD:top, :] = split(row)
    bh[n, top:, :], bl[n] = split((block - mean) * root)
    first = bh[n, 0 : top + HALF, :]
    second = bh[n, top + HALF :, :]
    left = mm_t(first, first[top:, :])
    right = mm_t(first, second)
    left_low = mm_t(first, bl[n, LO, :])
    right_low = mm_t(first, bl[n, HI, :])
    sums = {
        (0, 0): 0.5 * left[top:] + left_low[top:],
        (0, 1): right[top:] + right_low[top:],
        (1, 0): mm_t(second, bl[n, LO, :]),
        (1, 1): 0.5 * mm_t(second, second) + mm_t(second, bl[n, HI, :]),
    }
    for (a, b), value in sums.items():
        spot_a, spot_b = (LO, HI)[a], (LO, HI)[b]
        new[n, spot_a, spot_b] = value if old is None else value + old[n, spot_a, spot_b]
    for spot_b, high, low in ((LO, left, left_low), (HI, right, right_low)):
        rhs = jnp.broadcast_to(high[0:1] + high[PAD : PAD + 1] + low[0:1], (8, HALF))
        new_rhs[n, :, spot_b] = rhs if old_rhs is None else rhs + old_rhs[n, :, spot_b]


def part_kernel(spot, block_ref, wsum_ref, *refs):
    old, old_rhs = refs[:-4] if len(refs) == 6 else (None, None)
    new, new_rhs, bh, bl = refs[-4:]
    for n in range(new.shape[0]):
        add_part(n, spot, block_ref, wsum_ref, bh, bl, old, old_rhs, new, new_rhs)


def gram_part(which, block, wsum, members, sofar=()):
    patches, obs_tile = wsum.shape[0], block.shape[1]
    spot = slice(which * obs_tile, (which + 1) * obs_tile)
    return pl.pallas_call(
        functools.partial(part_kernel, spot),
        out_shape=(
            jax.ShapeDtypeStruct((patches, members, members), F32),
            jax.ShapeDtypeStruct((patches, 8, members), F32),
        ),
        scratch_shapes=[
            pltpu.VMEM((patches, 2 * PAD + members, obs_tile), BF),
            pltpu.VMEM((patches, members, obs_tile), BF),
        ],
        compiler_params=pltpu.CompilerParams(vmem_limit_bytes=24 * 1024 * 1024),
        cost_estimate=pl.CostEstimate(flops=2 * 10**9, bytes_accessed=4 * 10**6, transcendentals=0),
    )(block, wsum, *sofar)


def root_kernel(
    far_ref, wsum_ref, gram_ref, part_ref, high_ref, low_ref, weight_ref, rhs_ref, bh, bl, t, p, ph, pl_, gh, gl, z, zh, zl
):
    obs_tile = far_ref.shape[1]
    patches, members = high_ref.shape[:2]
    inv = 1.0 / (members - 1)
    eye = (
        lax.broadcasted_iota(jnp.int32, (HALF, HALF), 0)
        == lax.broadcasted_iota(jnp.int32, (HALF, HALF), 1)
    ).astype(F32)

    def put(value, full, high, low, n, rows, cols):
        if full is not None:
            full[n, rows, cols] = value
        high[n, rows, cols], low[n, rows, cols] = split(value)

    def gram(n):
        spot = slice(2 * obs_tile, 3 * obs_tile)
        add_part(n, spot, far_ref, wsum_ref, bh, bl, gram_ref, part_ref, t, rhs_ref)
        rhs_ref[n] = rhs_ref[n] * inv

    def start(n):
        g00 = (t[n, LO, LO] + t[n, LO, LO].T) * inv + eye
        g01 = (t[n, LO, HI] + t[n, HI, LO].T) * inv
        g11 = (t[n, HI, HI] + t[n, HI, HI].T) * inv + eye
        g10 = g01.T
        rows0 = jnp.sum(jnp.abs(g00), 0, keepdims=True) + jnp.sum(jnp.abs(g10), 0, keepdims=True)
        rows1 = jnp.sum(jnp.abs(g01), 0, keepdims=True) + jnp.sum(jnp.abs(g11), 0, keepdims=True)
        scale = jnp.max(jnp.maximum(rows0, rows1), axis=1, keepdims=True)
        shrink = 1.0 / scale
        for rows, cols, g in ((LO, LO, g00), (LO, HI, g01), (HI, LO, g10), (HI, HI, g11)):
            cur = g * shrink
            put(cur, p, ph, pl_, n, rows, cols)
            first = -0.5 * cur
            if rows == cols:
                first = first + 1.5 * eye
            put(first, z, zh, zl, n, rows, cols)
        return scale

    def square(n):
        t[n, LO, LO] = 0.5 * mm(ph[n, LO, :], ph[n, :, LO]) + mm(ph[n, LO, :], pl_[n, :, LO])
        t[n, HI, LO] = mm(ph[n, HI, :], ph[n, :, LO]) + mm(ph[n, HI, :], pl_[n, :, LO])
        t[n, LO, HI] = mm(ph[n, LO, :], pl_[n, :, HI])
        t[n, HI, HI] = 0.5 * mm(ph[n, HI, :], ph[n, :, HI]) + mm(ph[n, HI, :], pl_[n, :, HI])

    def squared(n, one_pass):
        g00 = t[n, LO, LO] + t[n, LO, LO].T
        g10 = t[n, HI, LO] + t[n, LO, HI].T
        g11 = t[n, HI, HI] + t[n, HI, HI].T
        for rows, cols, g in ((LO, LO, g00), (HI, LO, g10), (LO, HI, g10.T), (HI, HI, g11)):
            if one_pass:
                gh[n, rows, cols] = g.astype(BF)
            else:
                put(g, None, gh, gl, n, rows, cols)
        p[n, LO, LO] = 2.25 * p[n, LO, LO] - 1.5 * g00
        p[n, HI, LO] = 2.25 * p[n, HI, LO] - 1.5 * g10
        p[n, HI, HI] = 2.25 * p[n, HI, HI] - 1.5 * g11

    def product(n, high, low, rows, cols):
        return (
            mm(ph[n, rows, :], high[n, :, cols])
            + mm(pl_[n, rows, :], high[n, :, cols])
            + mm(ph[n, rows, :], low[n, :, cols])
        )

    def factor(n):
        z00 = 1.5 * z[n, LO, LO] - 0.5 * product(n, zh, zl, LO, LO)
        z10 = 1.5 * z[n, HI, LO] - 0.5 * product(n, zh, zl, HI, LO)
        z11 = 1.5 * z[n, HI, HI] - 0.5 * product(n, zh, zl, HI, HI)
        return z00, z10, z11

    def few_factor(n, lead):
        gl[n, LO, LO] = (z[n, LO, LO] - lead * eye).astype(BF)
        gl[n, HI, LO] = z[n, HI, LO].astype(BF)
        gl[n, LO, HI] = z[n, HI, LO].T.astype(BF)
        gl[n, HI, HI] = (z[n, HI, HI] - lead * eye).astype(BF)

        def moved(rows, cols):
            part = lead * p[n, rows, cols] + mm(ph[n, rows, :], gl[n, :, cols])
            return 1.5 * z[n, rows, cols] - 0.5 * part

        return moved(LO, LO), moved(HI, LO), moved(HI, HI)

    def keep(n, parts):
        z00, z10, z11 = parts
        put(z00, z, zh, zl, n, LO, LO)
        put(z10, z, zh, zl, n, HI, LO)
        put(z10.T, None, zh, zl, n, LO, HI)
        put(z11, z, zh, zl, n, HI, HI)

    def cube(n, one_pass):
        def times(rows, cols):
            if one_pass:
                return mm(ph[n, rows, :], gh[n, :, cols])
            return product(n, gh, gl, rows, cols)

        n00 = p[n, LO, LO] + 0.25 * times(LO, LO)
        n10 = p[n, HI, LO] + 0.25 * times(HI, LO)
        n11 = p[n, HI, HI] + 0.25 * times(HI, HI)
        put(n00, p, ph, pl_, n, LO, LO)
        put(n10, p, ph, pl_, n, HI, LO)
        put(n10.T, None, ph, pl_, n, LO, HI)
        put(n11, p, ph, pl_, n, HI, HI)

    def mean_square(n):
        p00, p10, p11 = p[n, LO, LO], p[n, HI, LO], p[n, HI, HI]
        return jnp.sum(p00 * p00 + 2.0 * (p10 * p10) + p11 * p11) * (1.0 / members)

    def near_one(n):
        e10 = -p[n, HI, LO]
        gh[n, LO, LO] = (eye - p[n, LO, LO]).astype(BF)
        gh[n, HI, LO] = e10.astype(BF)
        gh[n, LO, HI] = e10.T.astype(BF)
        gh[n, HI, HI] = (eye - p[n, HI, HI]).astype(BF)

    def near_factor(n):
        z00 = z[n, LO, LO] + 0.5 * mm(gh[n, LO, :], zh[n, :, LO])
        z10 = z[n, HI, LO] + 0.5 * mm(gh[n, HI, :], zh[n, :, LO])
        z11 = z[n, HI, HI] + 0.5 * mm(gh[n, HI, :], zh[n, :, HI])
        return z00, z10, z11

    def near_square(n):
        t[n, LO, LO] = mm(gh[n, LO, :], gh[n, :, LO])
        t[n, HI, LO] = mm(gh[n, HI, :], gh[n, :, LO])
        t[n, HI, HI] = mm(gh[n, HI, :], gh[n, :, HI])

    def near_squared(n):
        gl[n, LO, LO] = t[n, LO, LO].astype(BF)
        gl[n, HI, LO] = t[n, HI, LO].astype(BF)
        gl[n, LO, HI] = t[n, HI, LO].T.astype(BF)
        gl[n, HI, HI] = t[n, HI, HI].astype(BF)

    def near_cube(n):
        e00 = 0.75 * t[n, LO, LO] + 0.25 * mm(gh[n, LO, :], gl[n, :, LO])
        e10 = 0.75 * t[n, HI, LO] + 0.25 * mm(gh[n, HI, :], gl[n, :, LO])
        e11 = 0.75 * t[n, HI, HI] + 0.25 * mm(gh[n, HI, :], gl[n, :, HI])
        put(eye - e00, p, ph, pl_, n, LO, LO)
        put(-e10, p, ph, pl_, n, HI, LO)
        put(-e10.T, None, ph, pl_, n, LO, HI)
        put(eye - e11, p, ph, pl_, n, HI, HI)

    every = range(patches)
    for n in every:
        gram(n)
    scales = [start(n) for n in every]

    def sweep(lead, one_pass):
        for n in every:
            square(n)
        for n in every:
            if one_pass and lead is not None:
                keep(n, few_factor(n, lead))
            squared(n, one_pass)
            if not one_pass and lead is not None:
                keep(n, factor(n))
            cube(n, one_pass)

    def near_sweep(one_pass):
        for n in every:
            near_one(n)
        for n in every:
            near_square(n)
        for n in every:
            near_squared(n)
            keep(n, near_factor(n) if one_pass else factor(n))
            near_cube(n)

    least = jnp.min(1.0 / jnp.concatenate(scales, 0))
    mean = mean_square(0)
    for n in range(1, patches):
        mean = jnp.maximum(mean, mean_square(n))
    count = sum((mean <= bound).astype(jnp.int32) for bound in SMALL)
    count = jnp.where(least >= 1.0 / NARROW, count, 0)

    def onward(value):
        return 0.25 * value * (3.0 - value) * (3.0 - value)

    @pl.when(count == 0)
    def _():
        sweep(None, False)

    @pl.when(count > 0)
    def _():
        sweep(None, True)

    def step(k, carry):
        least, lead = carry
        few = k < count
        rest = jnp.logical_not(few)
        wide = 1.0 - least

        @pl.when(few)
        def _():
            sweep(lead, True)

        @pl.when(jnp.logical_and(rest, wide > MID))
        def _():
            sweep(lead, False)

        @pl.when(jnp.logical_and(rest, jnp.logical_and(wide <= MID, wide > LOW)))
        def _():
            near_sweep(False)

        @pl.when(jnp.logical_and(rest, wide <= LOW))
        def _():
            near_sweep(True)

        return onward(least), 1.5 * lead

    least, _ = lax.fori_loop(1, NS_ITERS - 1, step, (onward(least), jnp.float32(1.5)))

    def finish(make):
        for n in every:
            small = lax.rsqrt(scales[n])
            z00, z10, z11 = (part * small for part in make(n))
            first, last = rhs_ref[n, 0:1, LO], rhs_ref[n, 0:1, HI]
            for rows, parts in ((LO, (z00, z10.T)), (HI, (z10, z11))):
                for cols, part in zip((LO, HI), parts):
                    put(part, None, high_ref, low_ref, n, rows, cols)
                total = parts[0] * first + parts[1] * last
                weight_ref[n, rows, :] = jnp.sum(total, axis=1, keepdims=True)

    @pl.when(1.0 - least > LOW)
    def _():
        finish(factor)

    @pl.when(1.0 - least <= LOW)
    def _():
        for n in every:
            near_one(n)
        finish(near_factor)


def inverse_roots(near, own, far, wsum, members):
    sofar = gram_part(1, own, wsum, members)
    sofar = gram_part(0, near, wsum, members, sofar)
    patches, obs_tile = wsum.shape[0], far.shape[1]
    square = (patches, members, members)
    return pl.pallas_call(
        root_kernel,
        out_shape=(
            jax.ShapeDtypeStruct(square, BF),
            jax.ShapeDtypeStruct(square, BF),
            jax.ShapeDtypeStruct((patches, members, 1), F32),
            jax.ShapeDtypeStruct((patches, 8, members), F32),
        ),
        scratch_shapes=[
            pltpu.VMEM((patches, 2 * PAD + members, obs_tile), BF),
            pltpu.VMEM((patches, members, obs_tile), BF),
            pltpu.VMEM(square, F32),
            pltpu.VMEM(square, F32),
            pltpu.VMEM(square, BF),
            pltpu.VMEM(square, BF),
            pltpu.VMEM(square, BF),
            pltpu.VMEM(square, BF),
            pltpu.VMEM(square, F32),
            pltpu.VMEM(square, BF),
            pltpu.VMEM(square, BF),
        ],
        compiler_params=pltpu.CompilerParams(vmem_limit_bytes=28 * 1024 * 1024),
        cost_estimate=pl.CostEstimate(flops=25 * 10**9, bytes_accessed=4 * 10**6, transcendentals=0),
    )(far, wsum, *sofar)


def apply_kernel(high_ref, low_ref, weight_ref, cols_ref, out_ref):
    devices, patches, levels, mem_dev, nlat = cols_ref.shape
    members = devices * mem_dev
    for n in range(patches):
        high, low, weight = high_ref[n], low_ref[n], weight_ref[n]
        cols = jnp.concatenate(
            [cols_ref[:, n, lev].reshape(members, nlat) for lev in range(levels)], 1
        )
        center = jnp.sum(cols, axis=0, keepdims=True) * (1.0 / members)
        cols_high, cols_low = split(cols - center)
        moved = mm(high, cols_high) + mm(low, cols_high) + mm(high, cols_low)
        result = moved + (center + jnp.sum(moved * weight, axis=0, keepdims=True))
        for lev in range(levels):
            part = result[:, lev * nlat : (lev + 1) * nlat]
            out_ref[:, n, lev] = part.reshape(devices, mem_dev, nlat)


def apply_roots(high, low, weight, cols):
    return pl.pallas_call(
        apply_kernel,
        out_shape=jax.ShapeDtypeStruct(cols.shape, F32),
        compiler_params=pltpu.CompilerParams(vmem_limit_bytes=24 * 1024 * 1024),
        cost_estimate=pl.CostEstimate(flops=8 * 10**8, bytes_accessed=4 * 10**6, transcendentals=0),
    )(high, low, weight, cols)


def advance(field, west, courant):
    nlat = field.shape[1]
    lat = lax.broadcasted_iota(jnp.int32, field.shape, 1)
    upper = jnp.where(lat == nlat - 1, field, pltpu.roll(field, nlat - 1, 1))
    lower = jnp.where(lat == 0, field, pltpu.roll(field, 1, 1))
    return field - courant * (field - west) + DIFFUSE * (upper + lower - 2.0 * field)


def picker(cells, nlat):
    spot = (lax.broadcasted_iota(jnp.int32, (nlat, cells.shape[1]), 0) == cells % nlat).astype(BF)
    twice = jnp.concatenate([spot, spot], 0)
    return lambda value: mm(jnp.concatenate(split(value), 1), twice)


def inner_kernel(field_ref, pack_ref, out_ref, edge_ref, obs_ref):
    lines, levels, members, nlat = out_ref.shape
    cells = pack_ref[2:3, :].astype(jnp.int32)
    pick = picker(cells, nlat)
    source_row = cells // nlat
    obs = jnp.zeros(obs_ref.shape, F32)
    for lev in range(levels):
        courant = pack_ref[3:4, lev * nlat : (lev + 1) * nlat]
        old, old_next = None, None
        for line in range(lines):
            now = field_ref[pl.ds(lev * lines + line, members, stride=levels * lines), :]
            if line < NSTEP:
                edge_ref[line, lev] = now
            now_next = None
            if line >= 1:
                now_next = advance(now, old, courant)
            if line >= NSTEP:
                done = advance(now_next, old_next, courant)
                out_ref[line, lev] = done
                obs = jnp.where(source_row == lev * lines + line, pick(done), obs)
            old, old_next = now, now_next
    obs_ref[...] = obs


def inner_forecast(members, pack):
    mem_dev, levels, lines, nlat = members.shape
    rows = mem_dev * levels * lines
    return pl.pallas_call(
        inner_kernel,
        out_shape=(
            jax.ShapeDtypeStruct((lines, levels, mem_dev, nlat), F32),
            jax.ShapeDtypeStruct((NSTEP, levels, mem_dev, nlat), F32),
            jax.ShapeDtypeStruct((mem_dev, pack.shape[1]), F32),
        ),
        compiler_params=pltpu.CompilerParams(vmem_limit_bytes=24 * 1024 * 1024),
        cost_estimate=pl.CostEstimate(flops=10**8, bytes_accessed=2 * 10**6, transcendentals=0),
    )(members.reshape(rows, nlat), pack)


def edge_kernel(lines, halo_ref, edge_ref, pack_ref, partial_ref, field_ref, out_ref, message_ref):
    del field_ref
    _, levels, members, nlat = edge_ref.shape
    cells = pack_ref[2:3, :].astype(jnp.int32)
    pick = picker(cells, nlat)
    source_row = cells // nlat
    obs = partial_ref[...]
    for lev in range(levels):
        courant = pack_ref[3:4, lev * nlat : (lev + 1) * nlat]
        old = halo_ref[1, lev]
        old_next = advance(old, halo_ref[0, lev], courant)
        for line in range(NSTEP):
            now = edge_ref[line, lev]
            now_next = advance(now, old, courant)
            done = advance(now_next, old_next, courant)
            out_ref[line, lev] = done
            obs = jnp.where(source_row == lev * lines + line, pick(done), obs)
            old, old_next = now, now_next
    message_ref[...] = jnp.sqrt(pack_ref[1:2, :]) * (obs - pack_ref[0:1, :])


def edge_forecast(halo, edge, pack, partial, field):
    lines, levels, mem_dev, nlat = field.shape

    def whole(array):
        zeros = (0,) * array.ndim
        return pl.BlockSpec(array.shape, lambda i: zeros)

    first = pl.BlockSpec((NSTEP, levels, mem_dev, nlat), lambda i: (0, 0, 0, 0))
    small = (halo, edge, pack, partial)
    return pl.pallas_call(
        functools.partial(edge_kernel, lines),
        grid=(1,),
        out_shape=(
            jax.ShapeDtypeStruct(field.shape, F32),
            jax.ShapeDtypeStruct(partial.shape, F32),
        ),
        in_specs=[whole(a) for a in small] + [pl.BlockSpec(memory_space=pl.ANY)],
        out_specs=(first, whole(partial)),
        input_output_aliases={len(small): 0},
        compiler_params=pltpu.CompilerParams(vmem_limit_bytes=24 * 1024 * 1024),
        cost_estimate=pl.CostEstimate(flops=10**7, bytes_accessed=10**6, transcendentals=0),
    )(*small, field)


def restore_kernel(part_ref, out_hbm, out_ref, sems):
    devices, patches, levels, mem_dev, nlat = part_ref.shape
    lines = patches * devices
    group = 8
    copies = []
    for i in range(mem_dev // group):
        for device in range(devices):
            for n in range(patches):
                for lev in range(levels):
                    first = i * group * levels * lines + lev * lines + patches * device + n
                    rows = pl.ds(first, group, stride=levels * lines)
                    out_ref[rows, :] = part_ref[device, n, lev, i * group : (i + 1) * group, :]
        spot = pl.ds(i * group * levels * lines, group * levels * lines)
        copies.append(pltpu.make_async_copy(out_ref.at[spot], out_hbm.at[spot], sems.at[i]))
        copies[-1].start()
    for copy in copies:
        copy.wait()


def restore(parts):
    devices, patches, levels, mem_dev, nlat = parts.shape
    rows = mem_dev * levels * patches * devices
    out = pl.pallas_call(
        restore_kernel,
        out_shape=jax.ShapeDtypeStruct((rows, nlat), F32),
        in_specs=[pl.BlockSpec(memory_space=pltpu.VMEM)],
        out_specs=pl.BlockSpec(memory_space=pl.ANY),
        scratch_shapes=[
            pltpu.VMEM((rows, nlat), F32),
            pltpu.SemaphoreType.DMA((mem_dev // 8,)),
        ],
        compiler_params=pltpu.CompilerParams(vmem_limit_bytes=24 * 1024 * 1024),
    )(parts)
    return out.reshape(mem_dev, levels, patches * devices, nlat)


def shifted(value, axis, steps):
    count = lax.axis_size(axis)
    pairs = [(source, (source + steps) % count) for source in range(count)]
    return lax.ppermute(value, axis, pairs)


def neighbours(value):
    mem, tile = lax.axis_size("mem"), lax.axis_size("tile")
    pairs = [
        (m * tile + t, m * tile + (t + (1 if m % 2 == 0 else -1)) % tile)
        for m in range(mem)
        for t in range(tile)
    ]
    near = lax.ppermute(value, ("mem", "tile"), pairs)
    far = lax.ppermute(near, "mem", [(m, m ^ 1) for m in range(mem)])
    return near, far


def on_device(
    members, courant, obs_cell, obs_value, obs_rinv, nbr_obs, nbr_class, nbr_count, loc_table
):
    mem_dev, levels, lines, nlat = members.shape
    devices = lax.axis_size("mem")
    obs_tile = obs_cell.shape[0]
    slots = nbr_obs.shape[1]
    edge = jnp.transpose(members[:, :, lines - NSTEP :, :], (2, 1, 0, 3))
    halo = shifted(edge, "tile", 1)
    rows = [obs_value, obs_rinv, obs_cell.astype(F32), courant.reshape(-1)]
    pack = jnp.concatenate([row[None] for row in rows] + [jnp.zeros((4, obs_tile), F32)], 0)
    field, first_lines, partial = inner_forecast(members, pack)
    field, message = edge_forecast(halo, first_lines, pack, partial, field)
    own = lax.all_gather(message, "mem", axis=0, tiled=True)
    own, nbr_obs, nbr_class, nbr_count, loc_table, field = lax.optimization_barrier(
        (own, nbr_obs, nbr_class, nbr_count, loc_table, field)
    )
    near, far = neighbours(own)
    columns = lax.all_to_all(
        field.reshape(devices, lines // devices, levels, mem_dev, nlat), "mem", 0, 0, tiled=True
    )
    tile_index = lax.axis_index("tile")
    tile_count = lax.axis_size("tile")
    offset = (nbr_obs // obs_tile - tile_index + 1) % tile_count
    offset = jnp.where(lax.axis_index("mem") % 2 == 0, offset, 2 - offset)
    local_ids = offset * obs_tile + nbr_obs % obs_tile
    classes = jnp.arange(loc_table.shape[0])
    local_w = jnp.sum(jnp.where(nbr_class[..., None] == classes, loc_table, 0.0), -1)
    local_w = jnp.where(jnp.arange(slots) < nbr_count[:, None], local_w, 0.0)
    places = jnp.arange(3 * obs_tile)
    wsum = jnp.sum(jnp.where(local_ids[:, :, None] == places, local_w[:, :, None], 0.0), 1)

    high, low, weight, _ = inverse_roots(near, own, far, wsum, devices * mem_dev)
    parts = apply_roots(high, low, weight, columns)
    return restore(lax.all_to_all(parts, "mem", 0, 0, tiled=True))


def solution(mesh):
    return jax.shard_map(
        on_device,
        mesh=mesh,
        in_specs=(
            P("mem", None, "tile", None),
            P(),
            P("tile"),
            P("tile"),
            P("tile"),
            P(("tile", "mem"), None),
            P(("tile", "mem"), None),
            P(("tile", "mem")),
            P(),
        ),
        out_specs=P("mem", None, "tile", None),
        check_vma=False,
    )
```
